128 devices in a mesh: cache: 32 (over x, y, core), item: 4 (over z).
Axes of the slice: x: 4, y: 4, z: 4, core: 2. Of those that a mesh axis runs over, the one named last changes fastest.
Arguments:
- cand_items: int32 [32, 1024], P('cache'), may hold values from 0 to 8191
- item_table: bfloat16 [8192, 1024], P('item'), may hold values from -6 to 6
- kv_cache: bfloat16 [2048, 128, 16, 128], P('cache', None, 'item'), may hold values from -6 to 6
- hist_blocks: int32 [32, 64], replicated, may hold values from 0 to 2047, as said below
- pattern: int32 [32, 4, 64], P('cache'), may hold values 0 or 1
- w_query: bfloat16 [1024, 1024], P(None, 'item'), may hold values from -0.1875 to 0.1875
- w_gate: bfloat16 [1024, 1024], replicated, may hold values from -0.1875 to 0.1875
- norm_gain: float32 [1024], replicated, may hold values from 0.1 to 1.9
- w_out: bfloat16 [1024, 1024], replicated, may hold values from -0.1875 to 0.1875
Outputs:
- layer_out: bfloat16 [32, 1024, 1024], P('cache', 'item')
The draws below stay inside these ranges and needn't reach their ends.
Inputs may be any that keep to these rules, and one draw needn't show every extreme that they name: `hist_blocks`: entry b names a block held by index b // 64 of cache. The 64 blocks of one request are distinct, at most 4 of them are held by one index of cache, and every request has exactly 4 on some index.
All inputs are finite; a program needn't handle non-finite values. No bound on the sum of `pattern` on one device may be relied on, other than what follows from the above.
Results may differ from the reference program's by a relative error of at most 0.0046.
Values may be sent and summed in bfloat16 or wider, within the bound.
A program may use at most 128 MiB of HBM per device.

```python
import math
import jax
import jax.numpy as jnp
import numpy as np
from jax import lax

D = 1024
H = 16
DH = 64
BLK = 128
SLOT = 4
CB = 256
CAND = 1024
BLK_DEV = 64
REQS = 32
HB = 64
NBLK = 2048
ITEMS = 8192
CBLK = 4


def draw_hist_blocks(key, part):
    key = jax.random.fold_in(key, 11)
    subkeys = jax.random.split(key, 5)
    hot_owner = jax.random.randint(subkeys[0], (REQS,), 0, 4)
    jitter_draw = jax.random.randint(subkeys[1], (REQS, REQS, SLOT), 0, 2 ** 14)
    forced = jax.random.randint(subkeys[2], (REQS,), 0, REQS)
    boost_bits = (jnp.arange(REQS)[None, :] == forced[:, None]).astype(jnp.int32) * 2 ** 17
    priority = jitter_draw + hot_owner[None, :, None] * 2 ** 13 + boost_bits[:, :, None]
    priority_flat = priority.reshape(REQS, REQS * SLOT) * (REQS * SLOT) + jnp.arange(REQS * SLOT)[None, :]
    _, chosen = lax.top_k(priority_flat, HB)
    owner_of = chosen // SLOT
    copy_index = chosen % SLOT
    start_base = jax.random.randint(subkeys[3], (REQS, REQS), 0, BLK_DEV)
    first_block = jnp.take_along_axis(start_base, owner_of, axis=1)
    local_block = (first_block + copy_index) % BLK_DEV
    block_ids = owner_of * BLK_DEV + local_block
    order_keys = jax.random.randint(subkeys[4], (REQS, HB), 0, 2 ** 16) * HB + jnp.arange(HB)[None, :]
    permuted = jnp.argsort(order_keys, axis=1)
    return jnp.take_along_axis(block_ids, permuted, axis=1).astype(jnp.int32)


def touch_ends(drawn, key, least, largest):
    longest = drawn.shape.index(max(drawn.shape))
    spots = []
    for shift in (0, 1):
        where = [jax.random.randint(jax.random.fold_in(key, axis), (), 0, length) for axis, length in enumerate(drawn.shape)]
        where[longest] = (where[longest] + shift) % drawn.shape[longest]
        spots.append(tuple(where))
    return drawn.at[spots[0]].set(least).at[spots[1]].set(largest)


def steps_of(key, shape, cuts, least, top_value):
    loudness, own = 1.0, jax.random.fold_in(key, 6)
    for axis_at, blocks in cuts:
        heights = jnp.exp(jax.random.uniform(jax.random.fold_in(own, axis_at), (blocks,), jnp.float32, least / len(cuts), top_value / len(cuts)))
        loudness = loudness * jnp.repeat(heights, shape[axis_at] // blocks).reshape([-1 if axis == axis_at else 1 for axis in range(len(shape))])
    return loudness


def rank_bounds(number_of, skew):
    weights = [(1 << 20) // math.isqrt(rank ** skew) + 1 for rank in range(1, number_of + 1)]
    deviation = 1 + sum(weights) // (1 << 30)
    return np.cumsum(np.array([max(1, weight // deviation) for weight in weights]))


def ranked(own_key, dims, number_of, slope):
    listing = rank_bounds(number_of, slope)
    lot = jax.random.randint(jax.random.fold_in(own_key, 1), dims, 0, int(listing[number_of - 1]))
    standing = jnp.searchsorted(jnp.asarray(listing, jnp.int32), lot, side="right")
    return jax.random.permutation(jax.random.fold_in(own_key, 2), number_of)[standing].astype(jnp.int32)


def gaussian(rng, dims, scale, most, shards=(), kind=jnp.bfloat16):
    drawn = jax.random.normal(rng, dims, jnp.float32) * scale
    if len(shards) > 0:
        drawn = steps_of(rng, dims, shards, -0.22, 0.18) * drawn
    return jnp.clip(drawn, min=-most, max=most).astype(kind)


def setup_inputs(seed: int = 0) -> dict:
    key_of = jax.random.split(jax.random.key(seed), 10)
    cand_items = touch_ends(ranked(key_of[0], (REQS, CAND), ITEMS, 2), jax.random.fold_in(key_of[0], 3), 0, ITEMS - 1).astype(jnp.int32)
    item_table = gaussian(key_of[1], (ITEMS, D), 1.0, 6.0, ((0, 4),))
    kv_cache = gaussian(key_of[2], (NBLK, BLK, H, 2 * DH), 1.0, 6.0, ((0, 32), (2, 4)))
    hist_blocks = draw_hist_blocks(jax.random.fold_in(key_of[9], 71), 0)
    pattern = touch_ends((jax.random.randint(key_of[4], (REQS, CBLK, HB), 0, 4) < 3).astype(jnp.int32), jax.random.fold_in(key_of[4], 1), 0, 1)
    w_query = gaussian(key_of[5], (D, D), D ** -0.5, 0.1875, ((1, 4),))
    w_gate = gaussian(key_of[6], (D, D), D ** -0.5, 0.1875)
    norm_gain = jnp.clip(1.0 + 0.18 * jax.random.normal(key_of[7], (D,), jnp.float32), 0.1, 1.9)
    w_out = gaussian(key_of[8], (D, D), D ** -0.5, 0.1875)
    return dict(cand_items=cand_items, item_table=item_table, kv_cache=kv_cache, hist_blocks=hist_blocks, pattern=pattern, w_query=w_query, w_gate=w_gate, norm_gain=norm_gain, w_out=w_out)


def reference(cand_items, item_table, kv_cache, hist_blocks, pattern, w_query, w_gate, norm_gain, w_out):
    score_scale = DH ** (-0.5)

    def one_request(inputs):
        item_ids, block_ids, pattern_row = inputs
        embedded = jnp.take(item_table, item_ids, axis=0)
        queries = jax.nn.silu(jnp.dot(embedded, w_query, preferred_element_type=jnp.float32)).astype(jnp.bfloat16)
        gate_act = jax.nn.silu(jnp.dot(embedded, w_gate, preferred_element_type=jnp.float32))
        history = jnp.take(kv_cache, block_ids, axis=0).reshape(HB * BLK, H, 2 * DH).astype(jnp.float32)
        key_rows = history[:, :, :DH]
        value_rows = history[:, :, DH:]
        key_mask = jnp.repeat(pattern_row.astype(jnp.float32), BLK, axis=1)
        query_blocks = queries.reshape(CAND // CB, CB, H, DH).astype(jnp.float32)

        def one_block(block_in):
            query_block, mask_row = block_in
            scores = jnp.einsum('chd,khd->hck', query_block, key_rows) * score_scale
            weights = (jax.nn.silu(scores) * mask_row[None, None, :]).astype(jnp.bfloat16)
            return jnp.einsum('hck,khd->chd', weights.astype(jnp.float32), value_rows)
        attended = lax.map(one_block, (query_blocks, key_mask)).reshape(CAND, D)
        row_mean = lax.optimization_barrier(jnp.mean(attended, axis=1))
        row_var = lax.optimization_barrier(jnp.mean(attended * attended, axis=1)) - row_mean * row_mean
        normed = (attended - row_mean[:, None]) * lax.rsqrt(row_var + 1e-05)[:, None]
        hidden = (normed * norm_gain[None, :] * gate_act).astype(jnp.bfloat16)
        projected_rows = jnp.dot(hidden, w_out, preferred_element_type=jnp.float32)
        return (embedded.astype(jnp.float32) + projected_rows).astype(jnp.bfloat16)
    return lax.map(one_request, (cand_items, hist_blocks, pattern))
```

```python
import functools
import jax
import jax.numpy as jnp
from jax import lax
from jax.experimental import pallas as pl
from jax.experimental.pallas import tpu as pltpu
from jax.sharding import PartitionSpec as P

DH = 64
BLK = 128
SLOT = 4
CB = 256
RING = 4
SOURCES = 8
GROUP = 4
PHASES = ((2, 1), (3, 0))

norm_eps = 1e-05


def at(x, y, core):
    return ((x % RING) * RING + y % RING) * 2 + core


def kv_pairs(j, s):
    pairs = []
    for x in range(RING):
        for y in range(RING):
            for core in range(2):
                dest = at(x, y + j, 0) if core == s else at(x + j, y, 1)
                pairs.append((at(x, y, core), dest))
    return pairs


def ring_pairs(k):
    pairs = []
    for x in range(RING):
        for y in range(RING):
            pairs.append((at(x, y, 0), at(x + k, y, 0)))
            pairs.append((at(x, y, 1), at(x, y + k, 1)))
    return pairs


def pack_kernel(phases, here_ref, send_ref, kv_ref, *rest):
    outs, sems = rest[:-1], rest[-1]
    x, y, core = here_ref[0], here_ref[1], here_ref[2]

    def copies(run):
        for p, ks in enumerate(phases):
            for i in range(SOURCES):
                j, s = i // 2, i % 2
                same = core == s
                for kk, k in enumerate(ks):
                    rx = lax.rem(jnp.where(same, x + k, x + j), RING)
                    ry = lax.rem(jnp.where(same, y + j, y + k), RING)
                    request = (rx * RING + ry) * 2 + jnp.where(same, 0, 1)

                    def slot_step(slot, carry, p=p, i=i, kk=kk, k=k, request=request):
                        block = send_ref[request * SLOT + slot]

                        @pl.when(block >= 0)
                        def _():
                            run(
                                pltpu.make_async_copy(
                                    kv_ref.at[jnp.maximum(block, 0)],
                                    outs[p * SOURCES + i].at[kk, slot],
                                    sems.at[(i * RING + k) * SLOT + slot],
                                )
                            )

                        return carry

                    lax.fori_loop(0, SLOT, slot_step, 0)

    copies(lambda c: c.start())
    copies(lambda c: c.wait())


def pack(here, send, kv, phases):
    outs = []
    for ks in phases:
        outs += [jax.ShapeDtypeStruct((len(ks), SLOT) + kv.shape[1:], kv.dtype)] * SOURCES
    smem = pl.BlockSpec(memory_space=pltpu.SMEM)
    hbm = pl.BlockSpec(memory_space=pl.ANY)
    return pl.pallas_call(
        functools.partial(pack_kernel, phases),
        out_shape=outs,
        in_specs=[smem, smem, pl.BlockSpec(memory_space=pltpu.VMEM)],
        out_specs=[hbm] * len(outs),
        scratch_shapes=[pltpu.SemaphoreType.DMA((SOURCES * RING * SLOT,))],
        compiler_params=pltpu.CompilerParams(vmem_limit_bytes=40 * 2**20),
        cost_estimate=pl.CostEstimate(flops=0, bytes_accessed=16 * 2**20, transcendentals=0),
        name="pack",
    )(here, send, kv)


def attend_kernel(nk, cblks, heads, count_ref, list_ref, *rest):
    q_refs, kv_refs = rest[:nk], rest[nk : nk + SOURCES]
    o_refs = rest[nk + SOURCES : 2 * nk + SOURCES]
    held, queries, acc, sems = rest[2 * nk + SOURCES :]
    entries = SOURCES * SLOT
    stride = entries + GROUP

    def copy(k, i):
        return pltpu.make_async_copy(
            kv_refs[i].at[k], held.at[k, pl.ds(i * SLOT, SLOT)], sems.at[k * SOURCES + i]
        )

    for k in range(nk):
        for i in range(SOURCES):
            copy(k, i).start()
        held[k, entries] = jnp.zeros(held.shape[2:], held.dtype)
    for k in range(nk):
        for h in range(heads):
            queries[h] = q_refs[k][:, h * DH : (h + 1) * DH]
        for i in range(SOURCES):
            copy(k, i).wait()

        def one_cblk(c, carry, k=k):
            rows = pl.ds(pl.multiple_of(c * CB, CB), CB)
            acc[...] = jnp.zeros_like(acc)

            def group(g, carry):
                base = (k * cblks + c) * stride + g * GROUP
                ids = [list_ref[base + i] for i in range(GROUP)]
                kvs = [
                    jnp.concatenate([held[k, e, h] for e in ids], axis=0) for h in range(heads)
                ]
                halves = [
                    lax.dot_general(
                        queries[h, rows, :],
                        kvs[h][:, :DH],
                        (((1,), (1,)), ((), ())),
                        preferred_element_type=jnp.float32,
                    )
                    for h in range(heads)
                ]
                weights = [(s + s * jnp.tanh(s)).astype(jnp.bfloat16) for s in halves]
                for h in range(heads):
                    acc[h] += jnp.dot(weights[h], kvs[h], preferred_element_type=jnp.float32)
                return carry

            groups = (count_ref[k * cblks + c] + GROUP - 1) // GROUP
            lax.fori_loop(0, groups, group, 0)
            o_refs[k][rows, :] = jnp.concatenate(
                [acc[h][:, DH:] for h in range(heads)], axis=1
            ).astype(o_refs[k].dtype)
            return carry

        lax.fori_loop(0, cblks, one_cblk, 0)


def attend(counts, lists, qs, kvs):
    nk = len(qs)
    rows, width = qs[0].shape
    heads = width // DH
    cblks = rows // CB
    smem = pl.BlockSpec(memory_space=pltpu.SMEM)
    vmem = pl.BlockSpec(memory_space=pltpu.VMEM)
    hbm = pl.BlockSpec(memory_space=pl.ANY)
    entries = SOURCES * SLOT
    work = nk * cblks * heads * CB * BLK * entries
    return pl.pallas_call(
        functools.partial(attend_kernel, nk, cblks, heads),
        out_shape=[jax.ShapeDtypeStruct((rows, width), jnp.bfloat16)] * nk,
        in_specs=[smem, smem] + [vmem] * nk + [hbm] * SOURCES,
        out_specs=[vmem] * nk,
        scratch_shapes=[
            pltpu.VMEM((nk, entries + 1, heads, BLK, 2 * DH), jnp.bfloat16),
            pltpu.VMEM((heads, rows, DH), jnp.bfloat16),
            pltpu.VMEM((heads, CB, 2 * DH), jnp.float32),
            pltpu.SemaphoreType.DMA((nk * SOURCES,)),
        ],
        compiler_params=pltpu.CompilerParams(vmem_limit_bytes=40 * 2**20),
        cost_estimate=pl.CostEstimate(
            flops=16 * work * DH, bytes_accessed=nk * 6 * 2**20, transcendentals=work
        ),
        name="attend",
    )(counts, lists, *qs, *kvs)


def on_device(
    cand_items, item_table, kv_cache, hist_blocks, pattern, w_query, w_gate, norm_gain, w_out
):
    zs = lax.axis_size("item")
    z = lax.axis_index("item")
    me = lax.axis_index("cache")
    core, y, x = me % 2, (me // 2) % RING, me // (2 * RING)
    on0 = core == 0
    blocks_here = kv_cache.shape[0]
    list_len = hist_blocks.shape[1]
    width = w_gate.shape[0]
    ring = lambda d: [(i, (i + d) % zs) for i in range(zs)]

    owner_of = hist_blocks // blocks_here
    local_of = hist_blocks % blocks_here
    same_owner = owner_of[:, :, None] == owner_of[:, None, :]
    positions = jnp.arange(list_len)
    earlier = positions[None, :] < positions[:, None]
    slot_rank = jnp.sum(same_owner & earlier[None], axis=2)
    slots = jnp.arange(SLOT)
    selected = (owner_of == me)[:, None, :] & (slot_rank[:, None, :] == slots[None, :, None])
    send = jnp.sum(jnp.where(selected, local_of[:, None, :] + 1, 0), axis=2) - 1
    here = jnp.stack([x, y, core]).astype(jnp.int32)
    kv_heads = kv_cache.transpose(0, 2, 1, 3)
    packed = pack(here, send.reshape(-1).astype(jnp.int32), kv_heads, PHASES)
    arrived = []
    for p in range(len(PHASES)):
        for i in range(SOURCES):
            block = packed[p * SOURCES + i]
            arrived.append(block if i == 0 else lax.ppermute(block, "cache", kv_pairs(i // 2, i % 2)))

    item_ids = cand_items[0]
    table_rows = item_table.shape[0]
    rows_per = item_ids.shape[0] // zs

    def picked(d):
        ids = lax.dynamic_slice_in_dim(item_ids, ((z + d) % zs) * rows_per, rows_per, 0)
        local = ids - z * table_rows
        inside = (local >= 0) & (local < table_rows)
        taken = jnp.take(item_table, jnp.clip(local, 0, table_rows - 1), axis=0)
        return jnp.where(inside[:, None], taken, jnp.zeros((), taken.dtype))

    embedded = picked(0)
    for d in range(1, zs):
        embedded = embedded + lax.ppermute(picked(d), "item", ring(d))
    chunks = [embedded] + [lax.ppermute(embedded, "item", ring(d)) for d in range(1, zs)]
    queries = jax.nn.silu(
        jnp.dot(jnp.concatenate(chunks, axis=0), w_query, preferred_element_type=jnp.float32)
    ).astype(jnp.bfloat16)
    queries = queries * jnp.asarray(0.5 * DH ** (-0.5), jnp.bfloat16)
    q_of = {0: queries}
    for k in range(1, RING):
        q_of[k] = lax.ppermute(queries, "cache", ring_pairs(-k))

    pattern_all = lax.all_gather(pattern[0], "cache")
    sources = jnp.arange(SOURCES)
    src_j, src_s = sources // 2, sources % 2
    owner_idx = jnp.where(
        on0, at(x, y - src_j + RING, src_s), at(x - src_j + RING, y, 1 - src_s)
    )
    order = [k for ks in PHASES for k in ks]
    k_arr = jnp.array(order)
    request = jnp.where(on0, at(x + k_arr, y, 0), at(x, y + k_arr, 1))
    owner_k = owner_of[request]
    rank_k = slot_rank[request]
    rotation = (z - jnp.arange(zs)) % zs
    pattern_k = pattern_all[request][:, rotation]
    entry_of = jnp.sum(
        jnp.where(owner_k[:, None, :] == owner_idx[None, :, None], sources[None, :, None] + 1, 0), axis=1
    ) - 1
    entry_of = jnp.where(entry_of >= 0, entry_of * SLOT + rank_k, -1)
    wanted = (pattern_k != 0) & (entry_of >= 0)[:, None, :]
    before = jnp.sum(
        (wanted[:, :, None, :] & earlier[None, None]).astype(jnp.int32), axis=3
    )
    entries = SOURCES * SLOT
    places = jnp.arange(entries + GROUP)
    lists = entries + jnp.sum(
        jnp.where(
            wanted[:, :, None, :] & (before[:, :, None, :] == places[None, None, :, None]),
            entry_of[:, None, None, :] - entries,
            0,
        ),
        axis=3,
    )
    counts = jnp.sum(wanted.astype(jnp.int32), axis=2)

    partial = {}
    base = 0
    for p, ks in enumerate(PHASES):
        outs = attend(
            counts[base : base + len(ks)].reshape(-1).astype(jnp.int32),
            lists[base : base + len(ks)].reshape(-1).astype(jnp.int32),
            [q_of[k] for k in ks],
            arrived[p * SOURCES : (p + 1) * SOURCES],
        )
        base += len(ks)
        for k, o in zip(ks, outs):
            partial[k] = o
    attended = partial[0].astype(jnp.float32)
    for k in range(1, RING):
        attended = attended + lax.ppermute(partial[k], "cache", ring_pairs(k)).astype(jnp.float32)

    pieces = []
    for i in range(zs):
        piece = attended[i * rows_per : (i + 1) * rows_per]
        pieces.append(piece if i == 0 else lax.ppermute(piece, "item", ring(-i)))
    doubled = jnp.concatenate(pieces + pieces[:-1], axis=1)
    attended = lax.dynamic_slice_in_dim(doubled, ((zs - z) % zs) * pieces[0].shape[1], width, 1)

    gate_act = jax.nn.silu(jnp.dot(embedded, w_gate, preferred_element_type=jnp.float32))
    row_mean = jnp.mean(attended, axis=1, keepdims=True)
    row_var = jnp.mean(attended * attended, axis=1, keepdims=True) - row_mean * row_mean
    normed = (attended - row_mean) * lax.rsqrt(row_var + norm_eps)
    hidden = (normed * norm_gain[None, :] * gate_act).astype(jnp.bfloat16)
    projected = jnp.dot(hidden, w_out, preferred_element_type=jnp.float32)
    return (embedded.astype(jnp.float32) + projected).astype(jnp.bfloat16)[None]


def solution(mesh):
    placed = (
        P("cache", None),
        P("item", None),
        P("cache", None, "item", None),
        P(),
        P("cache", None, None),
        P(None, "item"),
        P(),
        P(),
        P(),
    )
    return jax.shard_map(
        on_device, mesh=mesh, in_specs=placed, out_specs=P("cache", "item", None), check_vma=False
    )
```

```python
import functools
import jax
import jax.numpy as jnp
from jax import lax
from jax.experimental import pallas as pl
from jax.experimental.pallas import tpu as pltpu
from jax.sharding import PartitionSpec as P

DH = 64
BLK = 128
SLOT = 4
CB = 256
RING = 4
SOURCES = 8
GROUP = 4
HOPS = (2, 1, 3)

norm_eps = 1e-05
MESH = pl.DeviceIdType.MESH


def at(x, y, core):
    return (lax.rem(x + 2 * RING, RING) * RING + lax.rem(y + 2 * RING, RING)) * 2 + core


def place():
    me = lax.axis_index("cache")
    core = lax.rem(me, 2)
    y = lax.rem(lax.div(me, 2), RING)
    x = lax.div(me, 2 * RING)
    return x, y, core


def ring_peer(k):
    x, y, core = place()
    return jnp.where(core == 0, at(x + k, y, 0), at(x, y + k, 1))


def kv_dest(i):
    x, y, core = place()
    j, s = lax.div(i, 2), lax.rem(i, 2)
    return jnp.where(core == s, at(x, y + j, 0), at(x + j, y, 1))


def kv_source(i):
    x, y, core = place()
    j, s = lax.div(i, 2), lax.rem(i, 2)
    return jnp.where(core == 0, at(x, y - j, s), at(x - j, y, 1 - s))


def kv_request(i, k):
    x, y, core = place()
    j, s = lax.div(i, 2), lax.rem(i, 2)
    return jnp.where(core == s, at(x + k, y + j, 0), at(x + j, y + k, 1))


def ring_pairs(k):
    pairs = []
    for x in range(RING):
        for y in range(RING):
            here = (x * RING + y) * 2
            pairs.append((here, ((x + k) % RING * RING + y) * 2))
            pairs.append((here + 1, (x * RING + (y + k) % RING) * 2 + 1))
    return pairs


def gather_kernel(
    zs, send_ref, ids_ref, kv_ref, table_ref, wq_ref, wg_ref,
    recv_ref, q_ref, embedded_ref, gate_ref,
    stage, turn, parts, parts_in, chunks, queries,
    kv_out, kv_in, z1_out, z1_in, z2_out, z2_in, q_out, q_in, own_sem,
):
    z = lax.axis_index("item")
    rows = embedded_ref.shape[0]
    peer_z = lambda d: lax.rem(z + d + zs, zs)

    barrier = pltpu.get_barrier_semaphore()
    for i in range(1, SOURCES):
        pl.semaphore_signal(barrier, inc=1, device_id={"cache": kv_source(i)}, device_id_type=MESH)
    for k in HOPS:
        pl.semaphore_signal(barrier, inc=1, device_id={"cache": ring_peer(k)}, device_id_type=MESH)
        pl.semaphore_signal(barrier, inc=1, device_id={"item": peer_z(k)}, device_id_type=MESH)
    pl.semaphore_wait(barrier, SOURCES - 1 + 2 * len(HOPS))

    side = turn.shape[0]
    heads = side // BLK
    to = lax.broadcasted_iota(jnp.int32, turn.shape, 0)
    of = lax.broadcasted_iota(jnp.int32, turn.shape, 1)
    turn[...] = jnp.where(
        of == lax.rem(to, BLK) * heads + lax.div(to, BLK), 1.0, 0.0
    ).astype(turn.dtype)

    def kv_copy(i, k):
        return pltpu.make_async_remote_copy(
            src_ref=stage.at[i, k],
            dst_ref=recv_ref.at[i, k],
            send_sem=kv_out.at[i * RING + k],
            recv_sem=kv_in.at[i * RING + k],
            device_id={"cache": kv_dest(i)},
            device_id_type=MESH,
        )

    def own_copy(k):
        return pltpu.make_async_copy(stage.at[0, k], recv_ref.at[0, k], kv_out.at[k])

    def send_blocks(k):
        def step(n, carry):
            i = lax.rem(n + 2, SOURCES)
            request = kv_request(i, k)
            for slot in range(SLOT):
                block = kv_ref[send_ref[request * SLOT + slot]]
                stage[i, k, slot] = jnp.dot(
                    turn[...], block, preferred_element_type=jnp.float32
                ).astype(stage.dtype)

            @pl.when(i == 0)
            def _():
                own_copy(k).start()

            @pl.when(i != 0)
            def _():
                kv_copy(i, k).start()

            return carry

        lax.fori_loop(0, SOURCES, step, 0)

    def z1_copy(d):
        return pltpu.make_async_remote_copy(
            src_ref=parts.at[d],
            dst_ref=parts_in.at[d - 1],
            send_sem=z1_out.at[d - 1],
            recv_sem=z1_in.at[d - 1],
            device_id={"item": peer_z(d)},
            device_id_type=MESH,
        )

    def z2_copy(d):
        return pltpu.make_async_remote_copy(
            src_ref=chunks.at[0],
            dst_ref=chunks.at[d],
            send_sem=z2_out.at[d - 1],
            recv_sem=z2_in.at[d - 1],
            device_id={"item": peer_z(d)},
            device_id_type=MESH,
        )

    def q_copy(k):
        return pltpu.make_async_remote_copy(
            src_ref=queries,
            dst_ref=q_ref.at[k],
            send_sem=q_out.at[k - 1],
            recv_sem=q_in.at[k - 1],
            device_id={"cache": ring_peer(-k)},
            device_id_type=MESH,
        )

    send_blocks(2)

    for d in HOPS + (0,):
        ids = ids_ref[d * rows : (d + 1) * rows, :]
        hot = ids == lax.broadcasted_iota(jnp.int32, (rows, table_ref.shape[0]), 1)
        parts[d] = jnp.dot(
            jnp.where(hot, 1.0, 0.0).astype(table_ref.dtype),
            table_ref[...],
            preferred_element_type=jnp.float32,
        ).astype(parts.dtype)
        if d != 0:
            z1_copy(d).start()

    send_blocks(1)

    for d in HOPS:
        z1_copy(d).wait_recv()
    embedded = parts[0] + parts_in[0] + parts_in[1] + parts_in[2]
    chunks[0] = embedded
    for d in HOPS:
        z2_copy(d).start()
    embedded_ref[...] = embedded

    send_blocks(3)
    send_blocks(0)

    def silu(v):
        return v * jax.nn.sigmoid(v)

    gate_ref[...] = silu(jnp.dot(embedded, wg_ref[...], preferred_element_type=jnp.float32))
    scale = 0.5 * DH ** (-0.5)
    for d in (0,) + HOPS:
        if d != 0:
            z2_copy(d).wait_recv()
        queries[d * rows : (d + 1) * rows, :] = (
            silu(jnp.dot(chunks[d], wq_ref[...], preferred_element_type=jnp.float32)).astype(
                queries.dtype
            )
            * jnp.asarray(scale, queries.dtype)
        )
    for k in HOPS:
        q_copy(k).start()
    own_q = pltpu.make_async_copy(queries, q_ref.at[0], own_sem.at[0])
    own_q.start()

    for d in HOPS:
        z1_copy(d).wait_send()
        z2_copy(d).wait_send()

    def drain(n, carry):
        i, k = lax.div(n, RING), lax.rem(n, RING)

        @pl.when(i == 0)
        def _():
            own_copy(k).wait()

        @pl.when(i != 0)
        def _():
            kv_copy(i, k).wait()

        return carry

    lax.fori_loop(0, SOURCES * RING, drain, 0)
    own_q.wait()
    for k in HOPS:
        q_copy(k).wait()


def gather(zs, send, ids, kv, table, w_query, w_gate):
    smem = pl.BlockSpec(memory_space=pltpu.SMEM)
    vmem = pl.BlockSpec(memory_space=pltpu.VMEM)
    hbm = pl.BlockSpec(memory_space=pl.ANY)
    rows = ids.shape[0] // zs
    width = table.shape[1]
    part = w_query.shape[1]
    dma = pltpu.SemaphoreType.DMA
    moved = (SOURCES, RING, SLOT) + kv.shape[1:]
    return pl.pallas_call(
        functools.partial(gather_kernel, zs),
        out_shape=[
            jax.ShapeDtypeStruct(moved, kv.dtype),
            jax.ShapeDtypeStruct((RING, zs * rows, part), kv.dtype),
            jax.ShapeDtypeStruct((rows, width), kv.dtype),
            jax.ShapeDtypeStruct((rows, width), jnp.float32),
        ],
        in_specs=[smem, vmem, vmem, vmem, vmem, vmem],
        out_specs=[hbm, hbm, vmem, vmem],
        scratch_shapes=[
            pltpu.VMEM(moved, kv.dtype),
            pltpu.VMEM((kv.shape[1], kv.shape[1]), kv.dtype),
            pltpu.VMEM((zs, rows, width), kv.dtype),
            pltpu.VMEM((zs - 1, rows, width), kv.dtype),
            pltpu.VMEM((zs, rows, width), kv.dtype),
            pltpu.VMEM((zs * rows, part), kv.dtype),
            dma((SOURCES * RING,)),
            dma((SOURCES * RING,)),
            dma((zs - 1,)),
            dma((zs - 1,)),
            dma((zs - 1,)),
            dma((zs - 1,)),
            dma((RING - 1,)),
            dma((RING - 1,)),
            dma((1,)),
        ],
        compiler_params=pltpu.CompilerParams(
            collective_id=0, has_side_effects=True, vmem_limit_bytes=56 * 2**20
        ),
        name="gather",
    )(send, ids, kv, table, w_query, w_gate)


def attend_kernel(cblks, heads, count_ref, list_ref, q_ref, kv_ref, o_ref, held, queries, acc, sems):
    nk = q_ref.shape[0]
    entries = SOURCES * SLOT
    stride = entries + GROUP

    def copy(k, i):
        return pltpu.make_async_copy(
            kv_ref.at[i, k], held.at[k, pl.ds(i * SLOT, SLOT)], sems.at[k * SOURCES + i]
        )

    for k in range(nk):
        for i in range(SOURCES):
            copy(k, i).start()
        held[k, entries] = jnp.zeros(held.shape[2:], held.dtype)
    for k in range(nk):
        for h in range(heads):
            queries[h] = q_ref[k, :, h * DH : (h + 1) * DH]
        for i in range(SOURCES):
            copy(k, i).wait()

        def one_cblk(c, carry, k=k):
            rows = pl.ds(pl.multiple_of(c * CB, CB), CB)
            acc[...] = jnp.zeros_like(acc)

            def group(g, carry):
                base = (k * cblks + c) * stride + g * GROUP
                ids = [list_ref[base + i] for i in range(GROUP)]
                kvs = [
                    jnp.concatenate([held[k, e, h] for e in ids], axis=0) for h in range(heads)
                ]
                halves = [
                    lax.dot_general(
                        queries[h, rows, :],
                        kvs[h][:, :DH],
                        (((1,), (1,)), ((), ())),
                        preferred_element_type=jnp.float32,
                    )
                    for h in range(heads)
                ]
                weights = [(s + s * jnp.tanh(s)).astype(jnp.bfloat16) for s in halves]
                for h in range(heads):
                    acc[h] += jnp.dot(weights[h], kvs[h], preferred_element_type=jnp.float32)
                return carry

            groups = (count_ref[k * cblks + c] + GROUP - 1) // GROUP
            lax.fori_loop(0, groups, group, 0)
            o_ref[k, rows, :] = jnp.concatenate(
                [acc[h][:, DH:] for h in range(heads)], axis=1
            ).astype(o_ref.dtype)
            return carry

        lax.fori_loop(0, cblks, one_cblk, 0)


def attend(counts, lists, qs, kvs):
    nk, rows, width = qs.shape
    heads = width // DH
    cblks = rows // CB
    smem = pl.BlockSpec(memory_space=pltpu.SMEM)
    vmem = pl.BlockSpec(memory_space=pltpu.VMEM)
    hbm = pl.BlockSpec(memory_space=pl.ANY)
    entries = SOURCES * SLOT
    work = nk * cblks * heads * CB * BLK * entries
    return pl.pallas_call(
        functools.partial(attend_kernel, cblks, heads),
        out_shape=jax.ShapeDtypeStruct(qs.shape, qs.dtype),
        in_specs=[smem, smem, vmem, hbm],
        out_specs=vmem,
        scratch_shapes=[
            pltpu.VMEM((nk, entries + 1, heads, BLK, 2 * DH), qs.dtype),
            pltpu.VMEM((heads, rows, DH), qs.dtype),
            pltpu.VMEM((heads, CB, 2 * DH), jnp.float32),
            pltpu.SemaphoreType.DMA((nk * SOURCES,)),
        ],
        compiler_params=pltpu.CompilerParams(vmem_limit_bytes=48 * 2**20),
        cost_estimate=pl.CostEstimate(
            flops=16 * work * DH, bytes_accessed=nk * 6 * 2**20, transcendentals=work
        ),
        name="attend",
    )(counts, lists, qs, kvs)


def finish_kernel(
    zs, o_ref, embedded_ref, gate_ref, gain_ref, w_ref, out_ref,
    sums_in, pieces, pieces_in, o_out, o_in, z_out, z_in,
):
    z = lax.axis_index("item")
    peer_z = lambda d: lax.rem(z + d + zs, zs)
    rows, width = out_ref.shape
    part = width // zs

    barrier = pltpu.get_barrier_semaphore()
    for k in HOPS:
        pl.semaphore_signal(barrier, inc=1, device_id={"cache": ring_peer(k)}, device_id_type=MESH)
        pl.semaphore_signal(barrier, inc=1, device_id={"item": peer_z(k)}, device_id_type=MESH)
    pl.semaphore_wait(barrier, 2 * len(HOPS))

    def o_copy(i, k):
        at_rows = pl.ds(i * rows, rows)
        return pltpu.make_async_remote_copy(
            src_ref=o_ref.at[k, at_rows],
            dst_ref=sums_in.at[k - 1, at_rows],
            send_sem=o_out.at[i * (RING - 1) + k - 1],
            recv_sem=o_in.at[i * (RING - 1) + k - 1],
            device_id={"cache": ring_peer(k)},
            device_id_type=MESH,
        )

    def z_copy(i):
        return pltpu.make_async_remote_copy(
            src_ref=pieces.at[i],
            dst_ref=pieces_in.at[i - 1],
            send_sem=z_out.at[i - 1],
            recv_sem=z_in.at[i - 1],
            device_id={"item": peer_z(-i)},
            device_id_type=MESH,
        )

    for i in HOPS + (0,):
        for k in HOPS:
            o_copy(i, k).start()
    for i in HOPS + (0,):
        total = o_ref[0, i * rows : (i + 1) * rows, :].astype(jnp.float32)
        for k in HOPS:
            o_copy(i, k).wait_recv()
            total += sums_in[k - 1, i * rows : (i + 1) * rows, :].astype(jnp.float32)
        pieces[i] = total
        if i != 0:
            z_copy(i).start()
    for i in HOPS:
        z_copy(i).wait_recv()
    attended = [pieces[0]] + [pieces_in[i - 1] for i in range(1, zs)]
    row_mean = sum(jnp.sum(a, axis=1, keepdims=True) for a in attended) / width
    row_square = sum(jnp.sum(a * a, axis=1, keepdims=True) for a in attended) / width
    scale = lax.rsqrt(row_square - row_mean * row_mean + norm_eps)
    total = embedded_ref[...].astype(jnp.float32)
    for i, a in enumerate(attended):
        cols = pl.ds(pl.multiple_of(peer_z(i) * part, part), part)
        hidden = (a - row_mean) * scale * gain_ref[:, cols] * gate_ref[:, cols]
        total += jnp.dot(
            hidden.astype(jnp.bfloat16), w_ref[cols, :], preferred_element_type=jnp.float32
        )
    out_ref[...] = total.astype(out_ref.dtype)
    for i in HOPS:
        z_copy(i).wait_send()
    for i in range(zs):
        for k in HOPS:
            o_copy(i, k).wait_send()


def finish(zs, sums, embedded, gate_act, norm_gain, w_out):
    vmem = pl.BlockSpec(memory_space=pltpu.VMEM)
    rows, width = embedded.shape
    dma = pltpu.SemaphoreType.DMA
    return pl.pallas_call(
        functools.partial(finish_kernel, zs),
        out_shape=jax.ShapeDtypeStruct(embedded.shape, embedded.dtype),
        in_specs=[vmem] * 5,
        out_specs=vmem,
        scratch_shapes=[
            pltpu.VMEM((RING - 1,) + sums.shape[1:], sums.dtype),
            pltpu.VMEM((zs, rows, width // zs), jnp.float32),
            pltpu.VMEM((zs - 1, rows, width // zs), jnp.float32),
            dma((zs * (RING - 1),)),
            dma((zs * (RING - 1),)),
            dma((zs - 1,)),
            dma((zs - 1,)),
        ],
        compiler_params=pltpu.CompilerParams(
            collective_id=1, has_side_effects=True, vmem_limit_bytes=32 * 2**20
        ),
        name="finish",
    )(sums, embedded, gate_act, norm_gain[None, :], w_out)


def on_device(
    cand_items, item_table, kv_cache, hist_blocks, pattern, w_query, w_gate, norm_gain, w_out
):
    zs = lax.axis_size("item")
    z = lax.axis_index("item")
    me = lax.axis_index("cache")
    blocks_here = kv_cache.shape[0]
    list_len = hist_blocks.shape[1]
    item_ids = cand_items[0]
    rows_per = item_ids.shape[0] // zs

    owner_of = hist_blocks // blocks_here
    local_of = hist_blocks % blocks_here
    same_owner = owner_of[:, :, None] == owner_of[:, None, :]
    positions = jnp.arange(list_len)
    earlier = positions[None, :] < positions[:, None]
    slot_rank = jnp.sum(same_owner & earlier[None], axis=2)
    slots = jnp.arange(SLOT)
    selected = (owner_of == me)[:, None, :] & (slot_rank[:, None, :] == slots[None, :, None])
    send = jnp.sum(jnp.where(selected, local_of[:, None, :], 0), axis=2)

    turned = lax.dynamic_slice_in_dim(
        jnp.concatenate([item_ids, item_ids]), z * rows_per, item_ids.shape[0], 0
    )
    local_ids = (turned - z * item_table.shape[0])[:, None]
    kv_rows = kv_cache.reshape(blocks_here, -1, kv_cache.shape[3])
    moved, queries, embedded, gate_act = gather(
        zs, send.reshape(-1).astype(jnp.int32), local_ids, kv_rows, item_table, w_query, w_gate
    )
    moved = moved.reshape(moved.shape[:3] + (-1, BLK, 2 * DH))

    ks = jnp.arange(RING)
    request = jnp.stack([ring_peer(k) for k in range(RING)])
    sources = jnp.arange(SOURCES)
    owner_idx = jnp.stack([kv_source(i) for i in range(SOURCES)])
    owner_k = owner_of[request]
    rank_k = slot_rank[request]
    rotation = (z - jnp.arange(zs)) % zs
    pattern_of = [pattern[0]] + [
        lax.ppermute(pattern[0], "cache", ring_pairs(-k)) for k in range(1, RING)
    ]
    pattern_k = jnp.stack(pattern_of)[:, rotation]
    entry_of = jnp.sum(
        jnp.where(owner_k[:, None, :] == owner_idx[None, :, None], sources[None, :, None] + 1, 0), axis=1
    ) - 1
    entry_of = jnp.where(entry_of >= 0, entry_of * SLOT + rank_k, -1)
    wanted = (pattern_k != 0) & (entry_of >= 0)[:, None, :]
    before = jnp.sum(
        (wanted[:, :, None, :] & earlier[None, None]).astype(jnp.int32), axis=3
    )
    entries = SOURCES * SLOT
    places = jnp.arange(entries + GROUP)
    lists = entries + jnp.sum(
        jnp.where(
            wanted[:, :, None, :] & (before[:, :, None, :] == places[None, None, :, None]),
            entry_of[:, None, None, :] - entries,
            0,
        ),
        axis=3,
    )
    counts = jnp.sum(wanted.astype(jnp.int32), axis=2)
    sums = attend(
        counts.reshape(-1).astype(jnp.int32), lists.reshape(-1).astype(jnp.int32), queries, moved
    )
    return finish(zs, sums, embedded, gate_act, norm_gain, w_out)[None]


def solution(mesh):
    placed = (
        P("cache", None),
        P("item", None),
        P("cache", None, "item", None),
        P(),
        P("cache", None, None),
        P(None, "item"),
        P(),
        P(),
        P(),
    )
    return jax.shard_map(
        on_device, mesh=mesh, in_specs=placed, out_specs=P("cache", "item", None), check_vma=False
    )
```

```python
import functools
import jax
import jax.numpy as jnp
from jax import lax
from jax.experimental import pallas as pl
from jax.experimental.pallas import tpu as pltpu
from jax.sharding import PartitionSpec as P

DH = 64
BLK = 128
SLOT = 4
CB = 256
RING = 4
SOURCES = 8
STEP = 256
HOPS = (2, 1, 3)
ORDER = (0, 2, 1, 3)

norm_eps = 1e-05
MESH = pl.DeviceIdType.MESH


def at(x, y, core):
    return (lax.rem(x + 2 * RING, RING) * RING + lax.rem(y + 2 * RING, RING)) * 2 + core


def place():
    me = lax.axis_index("cache")
    core = lax.rem(me, 2)
    y = lax.rem(lax.div(me, 2), RING)
    x = lax.div(me, 2 * RING)
    return x, y, core


def ring_peer(k):
    x, y, core = place()
    return jnp.where(core == 0, at(x + k, y, 0), at(x, y + k, 1))


def kv_dest(i):
    x, y, core = place()
    j, s = lax.div(i, 2), lax.rem(i, 2)
    return jnp.where(core == s, at(x, y + j, 0), at(x + j, y, 1))


def kv_source(i):
    x, y, core = place()
    j, s = lax.div(i, 2), lax.rem(i, 2)
    return jnp.where(core == 0, at(x, y - j, s), at(x - j, y, 1 - s))


def kv_request(i, k):
    x, y, core = place()
    j, s = lax.div(i, 2), lax.rem(i, 2)
    return jnp.where(core == s, at(x + k, y + j, 0), at(x + j, y + k, 1))


def ring_pairs(k):
    pairs = []
    for x in range(RING):
        for y in range(RING):
            here = (x * RING + y) * 2
            pairs.append((here, ((x + k) % RING * RING + y) * 2))
            pairs.append((here + 1, (x * RING + (y + k) % RING) * 2 + 1))
    return pairs


def layer_kernel(
    zs, send_ref, mask_ref, ids_ref, kv_ref, table_ref, wq_ref, wg_ref, gain_ref, wo_ref,
    recv_ref, out_ref,
    stage, turn, parts, parts_in, chunks, queries, gate, held, keys, acc, own, sums, sums_in, pieces, pieces_in,
    kv_out, kv_in, z1_out, z1_in, z2_out, z2_in, q_out, q_in, held_sem, o_out, o_in, z3_out, z3_in,
):
    z = lax.axis_index("item")
    rows, width = out_ref.shape
    part = width // zs
    heads = part // DH
    peer_z = lambda d: lax.rem(z + d + zs, zs)

    barrier = pltpu.get_barrier_semaphore()
    for i in range(1, SOURCES):
        pl.semaphore_signal(barrier, inc=1, device_id={"cache": kv_source(i)}, device_id_type=MESH)
    for k in HOPS:
        pl.semaphore_signal(barrier, inc=1, device_id={"cache": ring_peer(k)}, device_id_type=MESH)
        pl.semaphore_signal(barrier, inc=1, device_id={"item": peer_z(k)}, device_id_type=MESH)
    pl.semaphore_wait(barrier, SOURCES - 1 + 2 * len(HOPS))

    to = lax.broadcasted_iota(jnp.int32, turn.shape, 0)
    of = lax.broadcasted_iota(jnp.int32, turn.shape, 1)
    turn[...] = jnp.where(
        of == lax.rem(to, BLK) * heads + lax.div(to, BLK), 1.0, 0.0
    ).astype(turn.dtype)

    def kv_copy(i, k):
        return pltpu.make_async_remote_copy(
            src_ref=stage.at[i, k],
            dst_ref=recv_ref.at[i, k],
            send_sem=kv_out.at[i * RING + k],
            recv_sem=kv_in.at[i * RING + k],
            device_id={"cache": kv_dest(i)},
            device_id_type=MESH,
        )

    def own_copy(k):
        return pltpu.make_async_copy(stage.at[0, k], recv_ref.at[0, k], kv_out.at[k])

    def send_blocks(k):
        def step(n, carry):
            i = lax.rem(n + 2, SOURCES)
            request = kv_request(i, k)
            for slot in range(SLOT):
                block = kv_ref[send_ref[request * SLOT + slot]]
                by_head = jnp.dot(turn[...], block, preferred_element_type=jnp.float32)
                turned = by_head.T.astype(stage.dtype)
                by_head = by_head.astype(stage.dtype)
                for p in range(heads // 2):
                    stage[i, k, slot, p * BLK : (p + 1) * BLK, :] = jnp.concatenate(
                        [by_head[h * BLK : (h + 1) * BLK, :DH] for h in (2 * p, 2 * p + 1)], axis=1
                    )
                for h in range(heads):
                    first = heads // 2 * BLK + h * DH
                    stage[i, k, slot, first : first + DH, :] = turned[DH:, h * BLK : (h + 1) * BLK]

            @pl.when(i == 0)
            def _():
                own_copy(k).start()

            @pl.when(i != 0)
            def _():
                kv_copy(i, k).start()

            return carry

        lax.fori_loop(0, SOURCES, step, 0)

    def z1_copy(d):
        return pltpu.make_async_remote_copy(
            src_ref=parts.at[d],
            dst_ref=parts_in.at[d - 1],
            send_sem=z1_out.at[d - 1],
            recv_sem=z1_in.at[d - 1],
            device_id={"item": peer_z(d)},
            device_id_type=MESH,
        )

    def z2_copy(d):
        return pltpu.make_async_remote_copy(
            src_ref=chunks.at[0],
            dst_ref=chunks.at[d],
            send_sem=z2_out.at[d - 1],
            recv_sem=z2_in.at[d - 1],
            device_id={"item": peer_z(d)},
            device_id_type=MESH,
        )

    def q_copy(k):
        return pltpu.make_async_remote_copy(
            src_ref=queries.at[0],
            dst_ref=queries.at[k],
            send_sem=q_out.at[k - 1],
            recv_sem=q_in.at[k - 1],
            device_id={"cache": ring_peer(-k)},
            device_id_type=MESH,
        )

    def o_copy(k):
        return pltpu.make_async_remote_copy(
            src_ref=sums.at[k - 1],
            dst_ref=sums_in.at[k - 1],
            send_sem=o_out.at[k - 1],
            recv_sem=o_in.at[k - 1],
            device_id={"cache": ring_peer(k)},
            device_id_type=MESH,
        )

    def z3_copy(i):
        return pltpu.make_async_remote_copy(
            src_ref=pieces.at[i],
            dst_ref=pieces_in.at[i - 1],
            send_sem=z3_out.at[i - 1],
            recv_sem=z3_in.at[i - 1],
            device_id={"item": peer_z(-i)},
            device_id_type=MESH,
        )

    send_blocks(ORDER[0])

    for d in HOPS + (0,):
        ids = ids_ref[d * rows : (d + 1) * rows, :]
        hot = ids == lax.broadcasted_iota(jnp.int32, (rows, table_ref.shape[0]), 1)
        parts[d] = jnp.dot(
            jnp.where(hot, 1.0, 0.0).astype(table_ref.dtype),
            table_ref[...],
            preferred_element_type=jnp.float32,
        ).astype(parts.dtype)
        if d != 0:
            z1_copy(d).start()

    send_blocks(ORDER[1])

    for d in HOPS:
        z1_copy(d).wait_recv()
    chunks[0] = parts[0] + parts_in[0] + parts_in[1] + parts_in[2]
    for d in HOPS:
        z2_copy(d).start()

    send_blocks(ORDER[2])
    send_blocks(ORDER[3])

    def silu(v):
        return v * jax.nn.sigmoid(v)

    gate[...] = silu(jnp.dot(chunks[0], wg_ref[...], preferred_element_type=jnp.float32))
    scale = 0.5 * DH ** (-0.5)
    for d in (0,) + HOPS:
        if d != 0:
            z2_copy(d).wait_recv()
        queries[0, :, d * rows : (d + 1) * rows] = silu(
            lax.dot_general(
                wq_ref[...], chunks[d], (((1,), (1,)), ((), ())), preferred_element_type=jnp.float32
            )
        ).astype(queries.dtype) * jnp.asarray(scale, queries.dtype)
    for k in HOPS:
        q_copy(k).start()

    def unit(u):
        place_in = lax.div(u, SOURCES)
        k = jnp.int32(ORDER[0])
        for p in range(1, RING):
            k = jnp.where(place_in == p, ORDER[p], k)
        return lax.rem(lax.rem(u, SOURCES) + 2, SOURCES), k

    def fetch(u):
        i, k = unit(u)
        return pltpu.make_async_copy(recv_ref.at[i, k], held.at[lax.rem(u, 2)], held_sem.at[lax.rem(u, 2)])

    def start_fetch(u):
        i, k = unit(u)

        @pl.when(i == 0)
        def _():
            own_copy(k).wait()

        @pl.when(i != 0)
        def _():
            kv_copy(i, k).wait_recv()

        fetch(u).start()

    units = SOURCES * RING
    start_fetch(0)
    fetch(0).wait()

    def one_unit(u, carry):
        i, k = unit(u)
        n = lax.rem(u, SOURCES)
        buf = lax.rem(u, 2)

        @pl.when(u + 1 < units)
        def _():
            start_fetch(u + 1)

        @pl.when(n == 0)
        def _():
            acc[...] = jnp.zeros_like(acc)

            @pl.when(k != 0)
            def _():
                q_copy(k).wait_recv()

        for slot in range(SLOT):
            at_slot = slice(slot * BLK, (slot + 1) * BLK)
            for p in range(heads // 2):
                pair = held[buf, slot, p * BLK : (p + 1) * BLK, :]
                keys[2 * p, at_slot, :] = pair[:, :DH]
                keys[2 * p + 1, at_slot, :] = pair[:, DH:]
        wanted = [
            [mask_ref[((k * SOURCES + i) * zs + b) * SLOT + slot].astype(keys.dtype) for slot in range(SLOT)]
            for b in range(zs)
        ]

        def half_scores(h, t):
            return jnp.dot(
                keys[h, t * STEP : (t + 1) * STEP, :],
                queries[k, h * DH : (h + 1) * DH, :],
                preferred_element_type=jnp.float32,
            )

        def add_values(h, t, weights):
            first = heads // 2 * BLK + h * DH
            slots = range(t * STEP // BLK, (t + 1) * STEP // BLK)
            values = [held[buf, slot, first : first + DH, :] for slot in slots]
            for b in range(zs):
                cols = slice(b * rows, (b + 1) * rows)
                masked = jnp.concatenate([v * wanted[b][s] for s, v in zip(slots, values)], axis=1)
                acc[h * DH : (h + 1) * DH, cols] += jnp.dot(
                    masked, weights[:, cols], preferred_element_type=jnp.float32
                )

        steps = [(h, t) for h in range(heads) for t in range(SLOT * BLK // STEP)]
        scores = half_scores(*steps[0])
        for m, (h, t) in enumerate(steps):
            later = half_scores(*steps[m + 1]) if m + 1 < len(steps) else None
            add_values(h, t, (scores + scores * jnp.tanh(scores)).astype(keys.dtype))
            scores = later

        @pl.when((n == SOURCES - 1) & (k == 0))
        def _():
            own[...] = acc[...]

        @pl.when((n == SOURCES - 1) & (k != 0))
        def _():
            sums[k - 1] = acc[...].astype(sums.dtype)
            o_copy(k).start()

        @pl.when(u + 1 < units)
        def _():
            fetch(u + 1).wait()

        return carry

    lax.fori_loop(0, units, one_unit, 0)

    for k in ORDER[1:]:
        o_copy(k).wait_recv()
        if k != ORDER[3]:
            own[...] += sums_in[k - 1].astype(jnp.float32)
    mine = None
    for i in HOPS + (0,):
        cols = slice(i * rows, (i + 1) * rows)
        total = (own[:, cols] + sums_in[ORDER[3] - 1, :, cols].astype(jnp.float32)).T
        if i == 0:
            mine = total
        else:
            pieces[i] = total.astype(pieces.dtype)
            z3_copy(i).start()
    for i in HOPS:
        z3_copy(i).wait_recv()
    attended = [mine] + [pieces_in[i - 1].astype(jnp.float32) for i in range(1, zs)]
    row_mean = sum(jnp.sum(a, axis=1, keepdims=True) for a in attended) / width
    row_square = sum(jnp.sum(a * a, axis=1, keepdims=True) for a in attended) / width
    norm = lax.rsqrt(row_square - row_mean * row_mean + norm_eps)
    total = chunks[0].astype(jnp.float32)
    for i, a in enumerate(attended):
        cols = pl.ds(pl.multiple_of(peer_z(i) * part, part), part)
        hidden = (a - row_mean) * norm * gain_ref[:, cols] * gate[:, cols]
        total += jnp.dot(
            hidden.astype(jnp.bfloat16), wo_ref[cols, :], preferred_element_type=jnp.float32
        )
    out_ref[...] = total.astype(out_ref.dtype)

    for d in HOPS:
        z1_copy(d).wait_send()
        z2_copy(d).wait_send()
        z3_copy(d).wait_send()
        q_copy(d).wait_send()
        o_copy(d).wait_send()

    def drain(n, carry):
        kv_copy(lax.div(n, RING) + 1, lax.rem(n, RING)).wait_send()
        return carry

    lax.fori_loop(0, (SOURCES - 1) * RING, drain, 0)


def layer(zs, send, mask, ids, kv, table, w_query, w_gate, norm_gain, w_out):
    smem = pl.BlockSpec(memory_space=pltpu.SMEM)
    vmem = pl.BlockSpec(memory_space=pltpu.VMEM)
    hbm = pl.BlockSpec(memory_space=pl.ANY)
    cands = ids.shape[0]
    rows = cands // zs
    width = table.shape[1]
    part = w_query.shape[0]
    heads = part // DH
    kind = kv.dtype
    dma = pltpu.SemaphoreType.DMA
    moved = (SOURCES, RING, SLOT) + kv.shape[1:]
    return pl.pallas_call(
        functools.partial(layer_kernel, zs),
        out_shape=[jax.ShapeDtypeStruct(moved, kind), jax.ShapeDtypeStruct((rows, width), kind)],
        in_specs=[smem, smem] + [vmem] * 7,
        out_specs=[hbm, vmem],
        scratch_shapes=[
            pltpu.VMEM(moved, kind),
            pltpu.VMEM((kv.shape[1], kv.shape[1]), kind),
            pltpu.VMEM((zs, rows, width), kind),
            pltpu.VMEM((zs - 1, rows, width), kind),
            pltpu.VMEM((zs, rows, width), kind),
            pltpu.VMEM((RING, part, cands), kind),
            pltpu.VMEM((rows, width), jnp.float32),
            pltpu.VMEM((2, SLOT) + kv.shape[1:], kind),
            pltpu.VMEM((heads, SLOT * BLK, DH), kind),
            pltpu.VMEM((part, cands), jnp.float32),
            pltpu.VMEM((part, cands), jnp.float32),
            pltpu.VMEM((RING - 1, part, cands), kind),
            pltpu.VMEM((RING - 1, part, cands), kind),
            pltpu.VMEM((zs, rows, part), kind),
            pltpu.VMEM((zs - 1, rows, part), kind),
            dma((SOURCES * RING,)),
            dma((SOURCES * RING,)),
            dma((zs - 1,)),
            dma((zs - 1,)),
            dma((zs - 1,)),
            dma((zs - 1,)),
            dma((RING - 1,)),
            dma((RING - 1,)),
            dma((2,)),
            dma((RING - 1,)),
            dma((RING - 1,)),
            dma((zs - 1,)),
            dma((zs - 1,)),
        ],
        compiler_params=pltpu.CompilerParams(
            collective_id=0, has_side_effects=True, vmem_limit_bytes=60 * 2**20
        ),
        name="layer",
    )(send, mask, ids, kv, table, w_query, w_gate, norm_gain, w_out)[1]


def on_device(
    cand_items, item_table, kv_cache, hist_blocks, pattern, w_query, w_gate, norm_gain, w_out
):
    zs = lax.axis_size("item")
    z = lax.axis_index("item")
    me = lax.axis_index("cache")
    blocks_here = kv_cache.shape[0]
    list_len = hist_blocks.shape[1]
    item_ids = cand_items[0]
    rows_per = item_ids.shape[0] // zs

    owner_of = hist_blocks // blocks_here
    local_of = hist_blocks % blocks_here
    same_owner = owner_of[:, :, None] == owner_of[:, None, :]
    positions = jnp.arange(list_len)
    earlier = positions[None, :] < positions[:, None]
    slot_rank = jnp.sum(same_owner & earlier[None], axis=2)
    slots = jnp.arange(SLOT)
    selected = (owner_of == me)[:, None, :] & (slot_rank[:, None, :] == slots[None, :, None])
    send = jnp.sum(jnp.where(selected, local_of[:, None, :], 0), axis=2)

    turned = lax.dynamic_slice_in_dim(
        jnp.concatenate([item_ids, item_ids]), z * rows_per, item_ids.shape[0], 0
    )
    local_ids = (turned - z * item_table.shape[0])[:, None]
    kv_rows = kv_cache.reshape(blocks_here, -1, kv_cache.shape[3])

    request = jnp.stack([ring_peer(k) for k in range(RING)])
    owner_idx = jnp.stack([kv_source(i) for i in range(SOURCES)])
    rotation = (z - jnp.arange(zs)) % zs
    pattern_of = [pattern[0]] + [
        lax.ppermute(pattern[0], "cache", ring_pairs(-k)) for k in range(1, RING)
    ]
    pattern_k = jnp.stack(pattern_of)[:, rotation]
    from_source = owner_of[request][:, None, None, :] == owner_idx[None, :, None, None]
    in_slot = slot_rank[request][:, None, None, :] == slots[None, None, :, None]
    filled = from_source & in_slot
    mask = jnp.any(filled[:, :, None] & (pattern_k != 0)[:, None, :, None], axis=4)
    out = layer(
        zs,
        send.reshape(-1).astype(jnp.int32),
        mask.reshape(-1).astype(jnp.float32),
        local_ids,
        kv_rows,
        item_table,
        w_query.T,
        w_gate,
        norm_gain[None, :],
        w_out,
    )
    return out[None]


def solution(mesh):
    placed = (
        P("cache", None),
        P("item", None),
        P("cache", None, "item", None),
        P(),
        P("cache", None, None),
        P(None, "item"),
        P(),
        P(),
        P(),
    )
    return jax.shard_map(
        on_device, mesh=mesh, in_specs=placed, out_specs=P("cache", "item", None), check_vma=False
    )
```

```python
import functools
import jax
import jax.numpy as jnp
from jax import lax
from jax.experimental import pallas as pl
from jax.experimental.pallas import tpu as pltpu
from jax.sharding import PartitionSpec as P

DH = 64
BLK = 128
SLOT = 4
CB = 256
RING = 4
SOURCES = 8
STEP = 256
HOPS = (2, 1, 3)
ORDER = (0, 2, 1, 3)

norm_eps = 1e-05
MESH = pl.DeviceIdType.MESH


def at(x, y, core):
    return (lax.rem(x + 2 * RING, RING) * RING + lax.rem(y + 2 * RING, RING)) * 2 + core


def place():
    me = lax.axis_index("cache")
    core = lax.rem(me, 2)
    y = lax.rem(lax.div(me, 2), RING)
    x = lax.div(me, 2 * RING)
    return x, y, core


def ring_peer(k):
    x, y, core = place()
    return jnp.where(core == 0, at(x + k, y, 0), at(x, y + k, 1))


def kv_dest(i):
    x, y, core = place()
    j, s = lax.div(i, 2), lax.rem(i, 2)
    return jnp.where(core == s, at(x, y + j, 0), at(x + j, y, 1))


def kv_source(i):
    x, y, core = place()
    j, s = lax.div(i, 2), lax.rem(i, 2)
    return jnp.where(core == 0, at(x, y - j, s), at(x - j, y, 1 - s))


def kv_request(i, k):
    x, y, core = place()
    j, s = lax.div(i, 2), lax.rem(i, 2)
    return jnp.where(core == s, at(x + k, y + j, 0), at(x + j, y + k, 1))


def source_at(n):
    return jnp.where(n < 2, n + 2, jnp.where(n < 4, n + 4, jnp.where(n < 6, 5 - n, n - 2)))


def layer_kernel(
    zs, send_ref, where_ref, ids_ref, pattern_ref, gain_ref, kv_hbm, table_hbm, wq_hbm, wg_hbm, wo_hbm,
    recv_ref, out_ref,
    kv_ref, table_ref, wq_ref, wg_ref, wo_ref, wq_turned, pattern_in, patterns,
    stage, turn, parts, relay_in, parts_in, chunks, queries, gate, held, keys, acc, own, sums, sums_in,
    pieces, pieces_in,
    load_sem, pat_out, pat_in, pat_here, kv_out, kv_in, z1_out, z1_in, z2_out, z2_in, q_out, q_in, held_sem,
    o_out, o_in, z3_out, z3_in,
):
    z = lax.axis_index("item")
    rows, width = out_ref.shape
    part = width // zs
    heads = part // DH
    half = rows // 2
    peer_z = lambda d: lax.rem(z + d + zs, zs)

    loads = [
        pltpu.make_async_copy(src, dst, load_sem.at[n])
        for n, (src, dst) in enumerate(
            [(table_hbm, table_ref), (kv_hbm, kv_ref), (wq_hbm, wq_ref), (wg_hbm, wg_ref), (wo_hbm, wo_ref)]
        )
    ]
    for load in loads:
        load.start()

    barrier = pltpu.get_barrier_semaphore()
    for i in range(1, SOURCES):
        pl.semaphore_signal(barrier, inc=1, device_id={"cache": kv_source(i)}, device_id_type=MESH)
    for k in HOPS:
        pl.semaphore_signal(barrier, inc=1, device_id={"cache": ring_peer(k)}, device_id_type=MESH)
        pl.semaphore_signal(barrier, inc=1, device_id={"item": peer_z(k)}, device_id_type=MESH)
    pl.semaphore_wait(barrier, SOURCES - 1 + 2 * len(HOPS))

    to = lax.broadcasted_iota(jnp.int32, turn.shape, 0)
    of = lax.broadcasted_iota(jnp.int32, turn.shape, 1)
    turn[...] = jnp.where(
        of == lax.rem(to, BLK) * heads + lax.div(to, BLK), 1.0, 0.0
    ).astype(turn.dtype)

    def kv_copy(i, k):
        return pltpu.make_async_remote_copy(
            src_ref=stage.at[i, k],
            dst_ref=recv_ref.at[i, k],
            send_sem=kv_out.at[i * RING + k],
            recv_sem=kv_in.at[i * RING + k],
            device_id={"cache": kv_dest(i)},
            device_id_type=MESH,
        )

    def own_copy(k):
        return pltpu.make_async_copy(stage.at[0, k], recv_ref.at[0, k], kv_out.at[k])

    def send_blocks(k, first, last):
        def step(n, carry):
            i = source_at(n)
            request = kv_request(i, k)
            for slot in range(SLOT):
                block = kv_ref[send_ref[request * SLOT + slot]]
                by_head = jnp.dot(turn[...], block, preferred_element_type=jnp.float32)
                turned = by_head.T.astype(stage.dtype)
                by_head = by_head.astype(stage.dtype)
                for p in range(heads // 2):
                    stage[i, k, slot, p * BLK : (p + 1) * BLK, :] = jnp.concatenate(
                        [by_head[h * BLK : (h + 1) * BLK, :DH] for h in (2 * p, 2 * p + 1)], axis=1
                    )
                for h in range(heads):
                    first = heads // 2 * BLK + h * DH
                    stage[i, k, slot, first : first + DH, :] = turned[DH:, h * BLK : (h + 1) * BLK]

            @pl.when(i == 0)
            def _():
                own_copy(k).start()

            @pl.when(i != 0)
            def _():
                kv_copy(i, k).start()

            return carry

        lax.fori_loop(first, last, step, 0)

    halves = {1: pl.ds(0, half), -1: pl.ds(half, half)}

    def z_remote(src, dst, out_sem, in_sem, d):
        return pltpu.make_async_remote_copy(
            src_ref=src, dst_ref=dst, send_sem=out_sem, recv_sem=in_sem,
            device_id={"item": peer_z(d)}, device_id_type=MESH,
        )

    def relay_copy(way):
        n = 0 if way == 1 else 1
        return z_remote(
            parts.at[2, halves[way]], relay_in.at[n], z1_out.at[n], z1_in.at[n], way
        )

    def part_copy(way, h):
        n = 0 if way == 1 else 1
        sem = 2 + 2 * n + (0 if h == 1 else 1)
        return z_remote(
            parts.at[way % zs, halves[h]], parts_in.at[n, halves[h]], z1_out.at[sem], z1_in.at[sem], way
        )

    def chunk_copy(way, h):
        n = (0 if way == 1 else 2) + (0 if h == 1 else 1)
        return z_remote(
            chunks.at[0, halves[h]], chunks.at[way % zs, halves[h]], z2_out.at[n], z2_in.at[n], way
        )

    def pass_copy(way):
        n = 4 if way == 1 else 5
        return z_remote(
            chunks.at[way % zs, halves[way]], chunks.at[2, halves[way]], z2_out.at[n], z2_in.at[n], way
        )

    def pattern_copy(k):
        return pltpu.make_async_remote_copy(
            src_ref=pattern_ref,
            dst_ref=pattern_in.at[k - 1],
            send_sem=pat_out.at[k - 1],
            recv_sem=pat_in.at[k - 1],
            device_id={"cache": ring_peer(-k)},
            device_id_type=MESH,
        )

    def pattern_here(k):
        src = pattern_ref if k == 0 else pattern_in.at[k - 1]
        return pltpu.make_async_copy(src, patterns.at[k], pat_here.at[k])

    def q_copy(k):
        return pltpu.make_async_remote_copy(
            src_ref=queries.at[0],
            dst_ref=queries.at[k],
            send_sem=q_out.at[k - 1],
            recv_sem=q_in.at[k - 1],
            device_id={"cache": ring_peer(-k)},
            device_id_type=MESH,
        )

    def o_copy(k):
        return pltpu.make_async_remote_copy(
            src_ref=sums.at[k - 1],
            dst_ref=sums_in.at[k - 1],
            send_sem=o_out.at[k - 1],
            recv_sem=o_in.at[k - 1],
            device_id={"cache": ring_peer(k)},
            device_id_type=MESH,
        )

    def z3_copy(i):
        return pltpu.make_async_remote_copy(
            src_ref=pieces.at[i],
            dst_ref=pieces_in.at[i - 1],
            send_sem=z3_out.at[i - 1],
            recv_sem=z3_in.at[i - 1],
            device_id={"item": peer_z(-i)},
            device_id_type=MESH,
        )

    for k in HOPS:
        pattern_copy(k).start()
    pattern_here(0).start()

    def pick(d):
        block = peer_z(d)
        ids = ids_ref[:, pl.ds(pl.multiple_of(block * rows, rows), rows)] - z * table_ref.shape[0]
        ids = jnp.broadcast_to(ids, (8, rows)).T[:, :1]
        hot = ids == lax.broadcasted_iota(jnp.int32, (rows, table_ref.shape[0]), 1)
        parts[d] = jnp.dot(
            jnp.where(hot, 1.0, 0.0).astype(table_ref.dtype),
            table_ref[...],
            preferred_element_type=jnp.float32,
        ).astype(parts.dtype)

    loads[0].wait()
    pick(2)
    relay_copy(1).start()
    relay_copy(-1).start()
    pick(1)
    part_copy(1, -1).start()
    pick(3)
    part_copy(-1, 1).start()
    loads[1].wait()
    send_blocks(0, 0, SOURCES // 2)
    relay_copy(1).wait()
    parts[1, halves[1]] += relay_in[0]
    part_copy(1, 1).start()
    relay_copy(-1).wait()
    parts[3, halves[-1]] += relay_in[1]
    part_copy(-1, -1).start()
    pick(0)
    send_blocks(2, 0, SOURCES)
    for way in (1, -1):
        for h in (1, -1):
            part_copy(way, h).wait()
    chunks[0] = parts[0] + parts_in[0] + parts_in[1]
    for way in (1, -1):
        chunk_copy(way, way).start()
    for way in (1, -1):
        chunk_copy(way, -way).start()

    def silu(v):
        return v * jax.nn.sigmoid(v)

    for load in loads[2:]:
        load.wait()
    wq_turned[...] = wq_ref[...].astype(jnp.float32).T.astype(wq_turned.dtype)
    scale = 0.5 * DH ** (-0.5)

    def make_queries(d):
        queries[0, :, d * rows : (d + 1) * rows] = silu(
            lax.dot_general(
                wq_turned[...], chunks[d], (((1,), (1,)), ((), ())), preferred_element_type=jnp.float32
            )
        ).astype(queries.dtype) * jnp.asarray(scale, queries.dtype)

    make_queries(0)
    for way in (1, -1):
        chunk_copy(way, way).wait()
        pass_copy(way).start()
    send_blocks(1, 0, SOURCES)
    for way in (1, -1):
        chunk_copy(way, -way).wait()
    make_queries(1)
    make_queries(3)
    for way in (1, -1):
        pass_copy(way).wait()
    make_queries(2)
    for k in HOPS:
        q_copy(k).start()
    send_blocks(3, 0, SOURCES)
    send_blocks(0, SOURCES // 2, SOURCES)
    gate[...] = silu(jnp.dot(chunks[0], wg_ref[...], preferred_element_type=jnp.float32))
    for k in HOPS:
        pattern_copy(k).wait()
        pattern_here(k).start()
    for k in range(RING):
        pattern_here(k).wait()

    lead = SOURCES // 2

    def unit(u):
        group = lax.div(u + SOURCES - lead, SOURCES)
        k = jnp.where(group == 1, ORDER[1], jnp.where(group == 2, ORDER[2], ORDER[3]))
        k = jnp.where((group == 0) | (group == RING), 0, k)
        n = lax.rem(u + SOURCES - lead, SOURCES)
        n = jnp.where(group == 0, u, jnp.where(group == RING, u - (RING - 1) * SOURCES, n))
        return source_at(n), k

    def fetch(u):
        i, k = unit(u)
        return pltpu.make_async_copy(recv_ref.at[i, k], held.at[lax.rem(u, 2)], held_sem.at[lax.rem(u, 2)])

    def start_fetch(u):
        i, k = unit(u)

        @pl.when(i == 0)
        def _():
            own_copy(k).wait()

        @pl.when(i != 0)
        def _():
            kv_copy(i, k).wait_recv()

        fetch(u).start()

    units = SOURCES * RING
    own[...] = jnp.zeros_like(own)
    start_fetch(0)
    fetch(0).wait()

    def one_unit(u, carry):
        i, k = unit(u)
        n = lax.rem(u + SOURCES - lead, SOURCES)
        starts = (n == 0) | (u == 0)
        ends = (n == SOURCES - 1) | (u == units - 1)
        buf = lax.rem(u, 2)

        @pl.when(u + 1 < units)
        def _():
            start_fetch(u + 1)

        @pl.when(starts)
        def _():
            acc[...] = jnp.zeros_like(acc)

            @pl.when(k != 0)
            def _():
                q_copy(k).wait_recv()

        for slot in range(SLOT):
            at_slot = slice(slot * BLK, (slot + 1) * BLK)
            for p in range(heads // 2):
                pair = held[buf, slot, p * BLK : (p + 1) * BLK, :]
                keys[2 * p, at_slot, :] = pair[:, :DH]
                keys[2 * p + 1, at_slot, :] = pair[:, DH:]
        wanted = [[None] * SLOT for b in range(zs)]
        for slot in range(SLOT):
            spot = where_ref[(k * SOURCES + i) * SLOT + slot]
            filled = jnp.where(spot < pattern_ref.shape[1], 1, 0)
            spot = jnp.minimum(spot, pattern_ref.shape[1] - 1)
            for b in range(zs):
                wish = patterns[k, peer_z(-b), spot] * filled
                wanted[b][slot] = wish.astype(jnp.float32).astype(keys.dtype)

        def half_scores(h, t):
            return jnp.dot(
                keys[h, t * STEP : (t + 1) * STEP, :],
                queries[k, h * DH : (h + 1) * DH, :],
                preferred_element_type=jnp.float32,
            )

        def add_values(h, t, weights):
            first = heads // 2 * BLK + h * DH
            slots = range(t * STEP // BLK, (t + 1) * STEP // BLK)
            values = [held[buf, slot, first : first + DH, :] for slot in slots]
            for b in range(zs):
                cols = slice(b * rows, (b + 1) * rows)
                masked = jnp.concatenate([v * wanted[b][s] for s, v in zip(slots, values)], axis=1)
                acc[h * DH : (h + 1) * DH, cols] += jnp.dot(
                    masked, weights[:, cols], preferred_element_type=jnp.float32
                )

        steps = [(h, t) for h in range(heads) for t in range(SLOT * BLK // STEP)]
        scores = half_scores(*steps[0])
        for m, (h, t) in enumerate(steps):
            later = half_scores(*steps[m + 1]) if m + 1 < len(steps) else None
            add_values(h, t, (scores + scores * jnp.tanh(scores)).astype(keys.dtype))
            scores = later

        @pl.when(ends & (k == 0))
        def _():
            own[...] += acc[...]

        @pl.when(ends & (k != 0))
        def _():
            sums[k - 1] = acc[...].astype(sums.dtype)
            o_copy(k).start()

        @pl.when(u + 1 < units)
        def _():
            fetch(u + 1).wait()

        return carry

    lax.fori_loop(0, units, one_unit, 0)

    for k in ORDER[1:]:
        o_copy(k).wait_recv()
    mine = None
    for i in HOPS + (0,):
        cols = slice(i * rows, (i + 1) * rows)
        total = own[:, cols]
        for k in ORDER[1:]:
            total += sums_in[k - 1, :, cols].astype(jnp.float32)
        total = total.T
        if i == 0:
            mine = total
        else:
            pieces[i] = total.astype(pieces.dtype)
            z3_copy(i).start()
    for i in HOPS:
        z3_copy(i).wait_recv()
    attended = [mine] + [pieces_in[i - 1].astype(jnp.float32) for i in range(1, zs)]
    row_mean = sum(jnp.sum(a, axis=1, keepdims=True) for a in attended) / width
    row_square = sum(jnp.sum(a * a, axis=1, keepdims=True) for a in attended) / width
    norm = lax.rsqrt(row_square - row_mean * row_mean + norm_eps)
    total = chunks[0].astype(jnp.float32)
    for i, a in enumerate(attended):
        cols = pl.ds(pl.multiple_of(peer_z(i) * part, part), part)
        hidden = (a - row_mean) * norm * gain_ref[:, cols] * gate[:, cols]
        total += jnp.dot(
            hidden.astype(jnp.bfloat16), wo_ref[cols, :], preferred_element_type=jnp.float32
        )
    out_ref[...] = total.astype(out_ref.dtype)

    for d in HOPS:
        z3_copy(d).wait_send()
        q_copy(d).wait_send()
        o_copy(d).wait_send()

    def drain(n, carry):
        kv_copy(lax.div(n, RING) + 1, lax.rem(n, RING)).wait_send()
        return carry

    lax.fori_loop(0, (SOURCES - 1) * RING, drain, 0)


def layer(zs, send, where, ids, pattern, norm_gain, kv, table, w_query, w_gate, w_out):
    smem = pl.BlockSpec(memory_space=pltpu.SMEM)
    vmem = pl.BlockSpec(memory_space=pltpu.VMEM)
    hbm = pl.BlockSpec(memory_space=pl.ANY)
    cands = ids.shape[1]
    rows = cands // zs
    width = table.shape[1]
    part = w_query.shape[1]
    heads = part // DH
    kind = kv.dtype
    dma = pltpu.SemaphoreType.DMA
    moved = (SOURCES, RING, SLOT) + kv.shape[1:]
    return pl.pallas_call(
        functools.partial(layer_kernel, zs),
        out_shape=[jax.ShapeDtypeStruct(moved, kind), jax.ShapeDtypeStruct((rows, width), kind)],
        in_specs=[smem, smem, vmem, vmem, vmem] + [hbm] * 5,
        out_specs=[hbm, vmem],
        scratch_shapes=[
            pltpu.VMEM(kv.shape, kind),
            pltpu.VMEM(table.shape, kind),
            pltpu.VMEM(w_query.shape, kind),
            pltpu.VMEM(w_gate.shape, kind),
            pltpu.VMEM(w_out.shape, kind),
            pltpu.VMEM(w_query.shape[::-1], kind),
            pltpu.VMEM((RING - 1,) + pattern.shape, pattern.dtype),
            pltpu.SMEM((RING,) + pattern.shape, pattern.dtype),
            pltpu.VMEM(moved, kind),
            pltpu.VMEM((kv.shape[1], kv.shape[1]), kind),
            pltpu.VMEM((zs, rows, width), kind),
            pltpu.VMEM((2, rows // 2, width), kind),
            pltpu.VMEM((2, rows, width), kind),
            pltpu.VMEM((zs, rows, width), kind),
            pltpu.VMEM((RING, part, cands), kind),
            pltpu.VMEM((rows, width), jnp.float32),
            pltpu.VMEM((2, SLOT) + kv.shape[1:], kind),
            pltpu.VMEM((heads, SLOT * BLK, DH), kind),
            pltpu.VMEM((part, cands), jnp.float32),
            pltpu.VMEM((part, cands), jnp.float32),
            pltpu.VMEM((RING - 1, part, cands), kind),
            pltpu.VMEM((RING - 1, part, cands), kind),
            pltpu.VMEM((zs, rows, part), kind),
            pltpu.VMEM((zs - 1, rows, part), kind),
            dma((5,)),
            dma((RING - 1,)),
            dma((RING - 1,)),
            dma((RING,)),
            dma((SOURCES * RING,)),
            dma((SOURCES * RING,)),
            dma((6,)),
            dma((6,)),
            dma((6,)),
            dma((6,)),
            dma((RING - 1,)),
            dma((RING - 1,)),
            dma((2,)),
            dma((RING - 1,)),
            dma((RING - 1,)),
            dma((zs - 1,)),
            dma((zs - 1,)),
        ],
        compiler_params=pltpu.CompilerParams(
            collective_id=0, has_side_effects=True, vmem_limit_bytes=62 * 2**20
        ),
        name="layer",
    )(send, where, ids, pattern, norm_gain, kv, table, w_query, w_gate, w_out)[1]


def on_device(
    cand_items, item_table, kv_cache, hist_blocks, pattern, w_query, w_gate, norm_gain, w_out
):
    zs = lax.axis_size("item")
    me = lax.axis_index("cache")
    blocks_here = kv_cache.shape[0]
    list_len = hist_blocks.shape[1]
    owner_of = hist_blocks // blocks_here
    positions = jnp.arange(list_len)
    so_far = positions[None, :] <= positions[:, None]
    slots = jnp.arange(SLOT)
    mine = owner_of == me
    count = jnp.sum((mine[:, None, :] & so_far[None]).astype(jnp.int32), axis=2)
    chosen = mine[:, None, :] & (count[:, None, :] == slots[None, :, None] + 1)
    send = jnp.sum(jnp.where(chosen, hist_blocks[:, None, :] - me * blocks_here, 0), axis=2)

    request = jnp.stack([ring_peer(k) for k in range(RING)])
    owner_idx = jnp.stack([kv_source(i) for i in range(SOURCES)])
    held = owner_of[request][:, None, :] == owner_idx[None, :, None]
    count = jnp.sum((held[:, :, None, :] & so_far[None, None]).astype(jnp.int32), axis=3)
    where = jnp.sum((count[:, :, None, :] <= slots[None, None, :, None]).astype(jnp.int32), axis=3)
    out = layer(
        zs,
        send.reshape(-1),
        where.reshape(-1),
        cand_items,
        pattern[0],
        norm_gain[None, :],
        kv_cache.reshape(blocks_here, -1, kv_cache.shape[3]),
        item_table,
        w_query,
        w_gate,
        w_out,
    )
    return out[None]


def solution(mesh):
    placed = (
        P("cache", None),
        P("item", None),
        P("cache", None, "item", None),
        P(),
        P("cache", None, None),
        P(None, "item"),
        P(),
        P(),
        P(),
    )
    return jax.shard_map(
        on_device, mesh=mesh, in_specs=placed, out_specs=P("cache", "item", None), check_vma=False
    )
```

```python
import functools
import jax
import jax.numpy as jnp
from jax import lax
from jax.experimental import pallas as pl
from jax.experimental.pallas import tpu as pltpu
from jax.sharding import PartitionSpec as P

DH = 64
BLK = 128
SLOT = 4
CB = 256
RING = 4
SOURCES = 8
STEP = 256
AHEAD = 17
HOPS = (2, 1, 3)
ORDER = (0, 2, 1, 3)

norm_eps = 1e-05
MESH = pl.DeviceIdType.MESH


def at(x, y, core):
    return (lax.rem(x + 2 * RING, RING) * RING + lax.rem(y + 2 * RING, RING)) * 2 + core


def place():
    me = lax.axis_index("cache")
    core = lax.rem(me, 2)
    y = lax.rem(lax.div(me, 2), RING)
    x = lax.div(me, 2 * RING)
    return x, y, core


def ring_peer(k):
    x, y, core = place()
    return jnp.where(core == 0, at(x + k, y, 0), at(x, y + k, 1))


def kv_dest(i):
    x, y, core = place()
    j, s = lax.div(i, 2), lax.rem(i, 2)
    return jnp.where(core == s, at(x, y + j, 0), at(x + j, y, 1))


def kv_source(i):
    x, y, core = place()
    j, s = lax.div(i, 2), lax.rem(i, 2)
    return jnp.where(core == 0, at(x, y - j, s), at(x - j, y, 1 - s))


def kv_request(i, k):
    x, y, core = place()
    j, s = lax.div(i, 2), lax.rem(i, 2)
    return jnp.where(core == s, at(x + k, y + j, 0), at(x + j, y + k, 1))


def source_at(n):
    return jnp.where(n < 2, n + 2, jnp.where(n < 4, n + 4, jnp.where(n < 6, 5 - n, n - 2)))


def layer_kernel(
    zs, hist_ref, ids_ref, pattern_ref, gain_ref, kv_hbm, table_hbm, wq_hbm, wg_hbm, wo_hbm,
    recv_ref, out_ref,
    kv_ref, table_ref, wq_ref, wg_ref, wo_ref, wq_turned, pattern_in, patterns, plan, tables,
    stage, turn, parts, relay_in, parts_in, chunks, queries, gate, held, keys, acc, own, sums, sums_in,
    pieces, pieces_in,
    load_sem, plan_sem, pat_out, pat_in, pat_here, kv_out, kv_in, z1_out, z1_in, z2_out, z2_in, q_out, q_in, held_sem,
    o_out, o_in, z3_out, z3_in,
):
    z = lax.axis_index("item")
    rows, width = out_ref.shape
    part = width // zs
    heads = part // DH
    half = rows // 2
    peer_z = lambda d: lax.rem(z + d + zs, zs)

    loads = [
        pltpu.make_async_copy(src, dst, load_sem.at[n])
        for n, (src, dst) in enumerate(
            [(kv_hbm, kv_ref), (table_hbm, table_ref), (wq_hbm, wq_ref), (wg_hbm, wg_ref), (wo_hbm, wo_ref)]
        )
    ]
    for load in loads:
        load.start()

    listed = hist_ref[...]
    held_here = kv_hbm.shape[0]
    length = listed.shape[1]
    up_to = lax.broadcasted_iota(jnp.int32, (length, length), 0) <= lax.broadcasted_iota(
        jnp.int32, (length, length), 1
    )
    up_to = jnp.where(up_to, 1.0, 0.0)
    lane = lax.broadcasted_iota(jnp.int32, (SOURCES, plan.shape[2]), 1)
    row = lax.broadcasted_iota(jnp.int32, (SOURCES, 1), 0)
    me = lax.axis_index("cache")

    def count(found):
        return jnp.dot(jnp.where(found, 1.0, 0.0), up_to, preferred_element_type=jnp.float32)

    for g in range(listed.shape[0] // SOURCES):
        at_rows = slice(g * SOURCES, (g + 1) * SOURCES)
        some = listed[at_rows]
        found = lax.div(some, held_here) == me
        nth = count(found)
        table = jnp.zeros(lane.shape, jnp.int32)
        for slot in range(SLOT):
            block = jnp.where(found & (nth == slot + 1.0), some - me * held_here, 0)
            table = jnp.where(lane == slot, jnp.sum(block, axis=1, keepdims=True), table)
        plan[0, at_rows, :] = table
    source = jnp.zeros(row.shape, jnp.int32)
    for i in range(SOURCES):
        source = jnp.where(row == i, kv_source(i), source)
    for k in range(RING):
        request = me if k == 0 else ring_peer(k)
        some = jnp.broadcast_to(hist_ref[pl.ds(request, 1), :], (SOURCES, length))
        nth = count(lax.div(some, held_here) == source)
        table = jnp.zeros(lane.shape, jnp.int32)
        for slot in range(SLOT):
            spot = jnp.sum(jnp.where(nth <= slot, 1, 0), axis=1, keepdims=True)
            table = jnp.where(lane == slot, spot, table)
        plan[1, k * SOURCES : (k + 1) * SOURCES, :] = table
    plan_copy = pltpu.make_async_copy(plan, tables, plan_sem.at[0])
    plan_copy.start()

    barrier = pltpu.get_barrier_semaphore()
    for i in range(1, SOURCES):
        pl.semaphore_signal(barrier, inc=1, device_id={"cache": kv_source(i)}, device_id_type=MESH)
    for k in HOPS:
        pl.semaphore_signal(barrier, inc=1, device_id={"cache": ring_peer(k)}, device_id_type=MESH)
        pl.semaphore_signal(barrier, inc=1, device_id={"item": peer_z(k)}, device_id_type=MESH)
    pl.semaphore_wait(barrier, SOURCES - 1 + 2 * len(HOPS))

    to = lax.broadcasted_iota(jnp.int32, turn.shape, 0)
    of = lax.broadcasted_iota(jnp.int32, turn.shape, 1)
    turn[...] = jnp.where(
        of == lax.rem(to, BLK) * heads + lax.div(to, BLK), 1.0, 0.0
    ).astype(turn.dtype)

    def kv_copy(i, k):
        return pltpu.make_async_remote_copy(
            src_ref=stage.at[i, k],
            dst_ref=recv_ref.at[i, k],
            send_sem=kv_out.at[i * RING + k],
            recv_sem=kv_in.at[i * RING + k],
            device_id={"cache": kv_dest(i)},
            device_id_type=MESH,
        )

    def own_copy(k):
        return pltpu.make_async_copy(stage.at[0, k], recv_ref.at[0, k], kv_out.at[k])

    lead = SOURCES // 2

    def unit(u):
        group = lax.div(u + SOURCES - lead, SOURCES)
        k = jnp.where(group == 1, ORDER[1], jnp.where(group == 2, ORDER[2], ORDER[3]))
        k = jnp.where((group == 0) | (group == RING), 0, k)
        n = lax.rem(u + SOURCES - lead, SOURCES)
        n = jnp.where(group == 0, u, jnp.where(group == RING, u - (RING - 1) * SOURCES, n))
        return source_at(n), k

    def stage_unit(u):
        i, k = unit(u)
        request = kv_request(i, k)
        for slot in range(SLOT):
            block = kv_ref[tables[0, request, slot]]
            by_head = jnp.dot(turn[...], block, preferred_element_type=jnp.float32)
            turned = by_head.T.astype(stage.dtype)
            by_head = by_head.astype(stage.dtype)
            for p in range(heads // 2):
                stage[i, k, slot, p * BLK : (p + 1) * BLK, :] = jnp.concatenate(
                    [by_head[h * BLK : (h + 1) * BLK, :DH] for h in (2 * p, 2 * p + 1)], axis=1
                )
            for h in range(heads):
                first = heads // 2 * BLK + h * DH
                stage[i, k, slot, first : first + DH, :] = turned[DH:, h * BLK : (h + 1) * BLK]

    def send_unit(u):
        i, k = unit(u)

        @pl.when(i == 0)
        def _():
            own_copy(k).start()

        @pl.when(i != 0)
        def _():
            kv_copy(i, k).start()

    def each_unit(first, last, *does):
        def step(u, carry):
            for do in does:
                do(u)
            return carry

        lax.fori_loop(first, last, step, 0)

    def send_units(first, last):
        each_unit(first, last, stage_unit, send_unit)

    halves = {1: pl.ds(0, half), -1: pl.ds(half, half)}

    def z_remote(src, dst, out_sem, in_sem, d):
        return pltpu.make_async_remote_copy(
            src_ref=src, dst_ref=dst, send_sem=out_sem, recv_sem=in_sem,
            device_id={"item": peer_z(d)}, device_id_type=MESH,
        )

    def relay_copy(way):
        n = 0 if way == 1 else 1
        return z_remote(
            parts.at[2, halves[way]], relay_in.at[n], z1_out.at[n], z1_in.at[n], way
        )

    def part_copy(way, h):
        n = 0 if way == 1 else 1
        sem = 2 + 2 * n + (0 if h == 1 else 1)
        return z_remote(
            parts.at[way % zs, halves[h]], parts_in.at[n, halves[h]], z1_out.at[sem], z1_in.at[sem], way
        )

    def chunk_copy(way, h):
        n = (0 if way == 1 else 2) + (0 if h == 1 else 1)
        return z_remote(
            chunks.at[0, halves[h]], chunks.at[way % zs, halves[h]], z2_out.at[n], z2_in.at[n], way
        )

    def pass_copy(way):
        n = 4 if way == 1 else 5
        return z_remote(
            chunks.at[way % zs, halves[way]], chunks.at[2, halves[way]], z2_out.at[n], z2_in.at[n], way
        )

    def pattern_copy(k):
        return pltpu.make_async_remote_copy(
            src_ref=pattern_ref,
            dst_ref=pattern_in.at[k - 1],
            send_sem=pat_out.at[k - 1],
            recv_sem=pat_in.at[k - 1],
            device_id={"cache": ring_peer(-k)},
            device_id_type=MESH,
        )

    def pattern_here(k):
        src = pattern_ref if k == 0 else pattern_in.at[k - 1]
        return pltpu.make_async_copy(src, patterns.at[k], pat_here.at[k])

    def q_copy(k):
        return pltpu.make_async_remote_copy(
            src_ref=queries.at[0],
            dst_ref=queries.at[k],
            send_sem=q_out.at[k - 1],
            recv_sem=q_in.at[k - 1],
            device_id={"cache": ring_peer(-k)},
            device_id_type=MESH,
        )

    def o_copy(k):
        return pltpu.make_async_remote_copy(
            src_ref=sums.at[k - 1],
            dst_ref=sums_in.at[k - 1],
            send_sem=o_out.at[k - 1],
            recv_sem=o_in.at[k - 1],
            device_id={"cache": ring_peer(k)},
            device_id_type=MESH,
        )

    def z3_copy(i):
        return pltpu.make_async_remote_copy(
            src_ref=pieces.at[i],
            dst_ref=pieces_in.at[i - 1],
            send_sem=z3_out.at[i - 1],
            recv_sem=z3_in.at[i - 1],
            device_id={"item": peer_z(-i)},
            device_id_type=MESH,
        )

    for k in HOPS:
        pattern_copy(k).start()
    pattern_here(0).start()

    def pick(d):
        block = peer_z(d)
        ids = ids_ref[:, pl.ds(pl.multiple_of(block * rows, rows), rows)] - z * table_ref.shape[0]
        ids = jnp.broadcast_to(ids, (8, rows)).T[:, :1]
        hot = ids == lax.broadcasted_iota(jnp.int32, (rows, table_ref.shape[0]), 1)
        parts[d] = jnp.dot(
            jnp.where(hot, 1.0, 0.0).astype(table_ref.dtype),
            table_ref[...],
            preferred_element_type=jnp.float32,
        ).astype(parts.dtype)

    plan_copy.wait()
    loads[0].wait()
    send_units(0, 1)
    loads[1].wait()
    pick(2)
    relay_copy(1).start()
    relay_copy(-1).start()
    send_units(1, 2)
    pick(1)
    part_copy(1, -1).start()
    send_units(2, 3)
    pick(3)
    part_copy(-1, 1).start()
    send_units(3, 5)
    relay_copy(1).wait()
    parts[1, halves[1]] += relay_in[0]
    part_copy(1, 1).start()
    relay_copy(-1).wait()
    parts[3, halves[-1]] += relay_in[1]
    part_copy(-1, -1).start()
    pick(0)
    send_units(5, 9)
    for way in (1, -1):
        for h in (1, -1):
            part_copy(way, h).wait()
    chunks[0] = parts[0] + parts_in[0] + parts_in[1]
    for way in (1, -1):
        chunk_copy(way, way).start()
    for way in (1, -1):
        chunk_copy(way, -way).start()

    def silu(v):
        return v * jax.nn.sigmoid(v)

    for load in loads[2:]:
        load.wait()
    wq_turned[...] = wq_ref[...].astype(jnp.float32).T.astype(wq_turned.dtype)
    scale = 0.5 * DH ** (-0.5)

    def make_queries(d):
        queries[0, :, d * rows : (d + 1) * rows] = silu(
            lax.dot_general(
                wq_turned[...], chunks[d], (((1,), (1,)), ((), ())), preferred_element_type=jnp.float32
            )
        ).astype(queries.dtype) * jnp.asarray(scale, queries.dtype)

    make_queries(0)
    for way in (1, -1):
        chunk_copy(way, way).wait()
        pass_copy(way).start()
    send_units(9, AHEAD)
    each_unit(AHEAD, 20, stage_unit)
    for way in (1, -1):
        chunk_copy(way, -way).wait()
    make_queries(1)
    make_queries(3)
    each_unit(20, 28, stage_unit)
    for way in (1, -1):
        pass_copy(way).wait()
    make_queries(2)
    for k in HOPS:
        q_copy(k).start()
    each_unit(AHEAD, 28, send_unit)
    send_units(28, 32)
    gate[...] = silu(jnp.dot(chunks[0], wg_ref[...], preferred_element_type=jnp.float32))
    for k in HOPS:
        pattern_copy(k).wait()
        pattern_here(k).start()
    for k in range(RING):
        pattern_here(k).wait()

    def fetch(u):
        i, k = unit(u)
        return pltpu.make_async_copy(recv_ref.at[i, k], held.at[lax.rem(u, 2)], held_sem.at[lax.rem(u, 2)])

    def start_fetch(u):
        i, k = unit(u)

        @pl.when(i == 0)
        def _():
            own_copy(k).wait()

        @pl.when(i != 0)
        def _():
            kv_copy(i, k).wait_recv()

        fetch(u).start()

    units = SOURCES * RING
    own[...] = jnp.zeros_like(own)
    start_fetch(0)
    fetch(0).wait()

    def one_unit(u, carry):
        i, k = unit(u)

        n = lax.rem(u + SOURCES - lead, SOURCES)
        starts = (n == 0) | (u == 0)
        ends = (n == SOURCES - 1) | (u == units - 1)
        buf = lax.rem(u, 2)

        @pl.when(u + 1 < units)
        def _():
            start_fetch(u + 1)

        @pl.when(starts)
        def _():
            acc[...] = jnp.zeros_like(acc)

            @pl.when(k != 0)
            def _():
                q_copy(k).wait_recv()

        for slot in range(SLOT):
            at_slot = slice(slot * BLK, (slot + 1) * BLK)
            for p in range(heads // 2):
                pair = held[buf, slot, p * BLK : (p + 1) * BLK, :]
                keys[2 * p, at_slot, :] = pair[:, :DH]
                keys[2 * p + 1, at_slot, :] = pair[:, DH:]
        wanted = [[None] * SLOT for b in range(zs)]
        for slot in range(SLOT):
            spot = tables[1, k * SOURCES + i, slot]
            filled = jnp.where(spot < pattern_ref.shape[1], 1, 0)
            spot = jnp.minimum(spot, pattern_ref.shape[1] - 1)
            for b in range(zs):
                wish = patterns[k, peer_z(-b), spot] * filled
                wanted[b][slot] = wish.astype(jnp.float32).astype(keys.dtype)

        def half_scores(h, t):
            return jnp.dot(
                keys[h, t * STEP : (t + 1) * STEP, :],
                queries[k, h * DH : (h + 1) * DH, :],
                preferred_element_type=jnp.float32,
            )

        def add_values(h, t, weights):
            first = heads // 2 * BLK + h * DH
            slots = range(t * STEP // BLK, (t + 1) * STEP // BLK)
            values = [held[buf, slot, first : first + DH, :] for slot in slots]
            for b in range(zs):
                cols = slice(b * rows, (b + 1) * rows)
                masked = jnp.concatenate([v * wanted[b][s] for s, v in zip(slots, values)], axis=1)
                acc[h * DH : (h + 1) * DH, cols] += jnp.dot(
                    masked, weights[:, cols], preferred_element_type=jnp.float32
                )

        steps = [(h, t) for h in range(heads) for t in range(SLOT * BLK // STEP)]
        scores = half_scores(*steps[0])
        for m, (h, t) in enumerate(steps):
            later = half_scores(*steps[m + 1]) if m + 1 < len(steps) else None
            add_values(h, t, (scores + scores * jnp.tanh(scores)).astype(keys.dtype))
            scores = later

        @pl.when(ends & (k == 0))
        def _():
            own[...] += acc[...]

        @pl.when(ends & (k != 0))
        def _():
            sums[k - 1] = acc[...].astype(sums.dtype)
            o_copy(k).start()

        @pl.when(u + 1 < units)
        def _():
            fetch(u + 1).wait()

        return carry

    lax.fori_loop(0, units, one_unit, 0)

    for k in ORDER[1:]:
        o_copy(k).wait_recv()
    mine = None
    for i in HOPS + (0,):
        cols = slice(i * rows, (i + 1) * rows)
        total = own[:, cols]
        for k in ORDER[1:]:
            total += sums_in[k - 1, :, cols].astype(jnp.float32)
        total = total.T
        if i == 0:
            mine = total
        else:
            pieces[i] = total.astype(pieces.dtype)
            z3_copy(i).start()
    for i in HOPS:
        z3_copy(i).wait_recv()
    attended = [mine] + [pieces_in[i - 1].astype(jnp.float32) for i in range(1, zs)]
    row_mean = sum(jnp.sum(a, axis=1, keepdims=True) for a in attended) / width
    row_square = sum(jnp.sum(a * a, axis=1, keepdims=True) for a in attended) / width
    norm = lax.rsqrt(row_square - row_mean * row_mean + norm_eps)
    total = chunks[0].astype(jnp.float32)
    for i, a in enumerate(attended):
        cols = pl.ds(pl.multiple_of(peer_z(i) * part, part), part)
        hidden = (a - row_mean) * norm * gain_ref[:, cols] * gate[:, cols]
        total += jnp.dot(
            hidden.astype(jnp.bfloat16), wo_ref[cols, :], preferred_element_type=jnp.float32
        )
    out_ref[...] = total.astype(out_ref.dtype)

    for d in HOPS:
        z3_copy(d).wait_send()
        q_copy(d).wait_send()
        o_copy(d).wait_send()

    def drain(n, carry):
        kv_copy(lax.div(n, RING) + 1, lax.rem(n, RING)).wait_send()
        return carry

    lax.fori_loop(0, (SOURCES - 1) * RING, drain, 0)


def layer(zs, hist, ids, pattern, norm_gain, kv, table, w_query, w_gate, w_out):
    vmem = pl.BlockSpec(memory_space=pltpu.VMEM)
    hbm = pl.BlockSpec(memory_space=pl.ANY)
    cands = ids.shape[1]
    rows = cands // zs
    width = table.shape[1]
    part = w_query.shape[1]
    heads = part // DH
    kind = kv.dtype
    dma = pltpu.SemaphoreType.DMA
    moved = (SOURCES, RING, SLOT) + kv.shape[1:]
    return pl.pallas_call(
        functools.partial(layer_kernel, zs),
        out_shape=[jax.ShapeDtypeStruct(moved, kind), jax.ShapeDtypeStruct((rows, width), kind)],
        in_specs=[vmem] * 4 + [hbm] * 5,
        out_specs=[hbm, vmem],
        scratch_shapes=[
            pltpu.VMEM(kv.shape, kind),
            pltpu.VMEM(table.shape, kind),
            pltpu.VMEM(w_query.shape, kind),
            pltpu.VMEM(w_gate.shape, kind),
            pltpu.VMEM(w_out.shape, kind),
            pltpu.VMEM(w_query.shape[::-1], kind),
            pltpu.VMEM((RING - 1,) + pattern.shape, pattern.dtype),
            pltpu.SMEM((RING,) + pattern.shape, pattern.dtype),
            pltpu.VMEM((2, RING * SOURCES, 128), jnp.int32),
            pltpu.SMEM((2, RING * SOURCES, 128), jnp.int32),
            pltpu.VMEM(moved, kind),
            pltpu.VMEM((kv.shape[1], kv.shape[1]), kind),
            pltpu.VMEM((zs, rows, width), kind),
            pltpu.VMEM((2, rows // 2, width), kind),
            pltpu.VMEM((2, rows, width), kind),
            pltpu.VMEM((zs, rows, width), kind),
            pltpu.VMEM((RING, part, cands), kind),
            pltpu.VMEM((rows, width), jnp.float32),
            pltpu.VMEM((2, SLOT) + kv.shape[1:], kind),
            pltpu.VMEM((heads, SLOT * BLK, DH), kind),
            pltpu.VMEM((part, cands), jnp.float32),
            pltpu.VMEM((part, cands), jnp.float32),
            pltpu.VMEM((RING - 1, part, cands), kind),
            pltpu.VMEM((RING - 1, part, cands), kind),
            pltpu.VMEM((zs, rows, part), kind),
            pltpu.VMEM((zs - 1, rows, part), kind),
            dma((5,)),
            dma((1,)),
            dma((RING - 1,)),
            dma((RING - 1,)),
            dma((RING,)),
            dma((SOURCES * RING,)),
            dma((SOURCES * RING,)),
            dma((6,)),
            dma((6,)),
            dma((6,)),
            dma((6,)),
            dma((RING - 1,)),
            dma((RING - 1,)),
            dma((2,)),
            dma((RING - 1,)),
            dma((RING - 1,)),
            dma((zs - 1,)),
            dma((zs - 1,)),
        ],
        compiler_params=pltpu.CompilerParams(
            collective_id=0, has_side_effects=True, vmem_limit_bytes=62 * 2**20
        ),
        name="layer",
    )(hist, ids, pattern, norm_gain, kv, table, w_query, w_gate, w_out)[1]


def on_device(
    cand_items, item_table, kv_cache, hist_blocks, pattern, w_query, w_gate, norm_gain, w_out
):
    zs = lax.axis_size("item")
    out = layer(
        zs,
        hist_blocks,
        cand_items,
        pattern[0],
        norm_gain[None, :],
        kv_cache.reshape(kv_cache.shape[0], -1, kv_cache.shape[3]),
        item_table,
        w_query,
        w_gate,
        w_out,
    )
    return out[None]


def solution(mesh):
    placed = (
        P("cache", None),
        P("item", None),
        P("cache", None, "item", None),
        P(),
        P("cache", None, None),
        P(None, "item"),
        P(),
        P(),
        P(),
    )
    return jax.shard_map(
        on_device, mesh=mesh, in_specs=placed, out_specs=P("cache", "item", None), check_vma=False
    )
```

```python
import functools
import jax
import jax.numpy as jnp
from jax import lax
from jax.experimental import pallas as pl
from jax.experimental.pallas import tpu as pltpu
from jax.sharding import PartitionSpec as P

DH = 64
BLK = 128
SLOT = 4
CB = 256
RING = 4
SOURCES = 8
STEP = 256
AHEAD = 17
HOPS = (2, 1, 3)
ORDER = (0, 2, 1, 3)

norm_eps = 1e-05
MESH = pl.DeviceIdType.MESH


def at(x, y, core):
    return (lax.rem(x + 2 * RING, RING) * RING + lax.rem(y + 2 * RING, RING)) * 2 + core


def place():
    me = lax.axis_index("cache")
    core = lax.rem(me, 2)
    y = lax.rem(lax.div(me, 2), RING)
    x = lax.div(me, 2 * RING)
    return x, y, core


def ring_peer(k):
    x, y, core = place()
    return jnp.where(core == 0, at(x + k, y, 0), at(x, y + k, 1))


def kv_dest(i):
    x, y, core = place()
    j, s = lax.div(i, 2), lax.rem(i, 2)
    return jnp.where(core == s, at(x, y + j, 0), at(x + j, y, 1))


def kv_source(i):
    x, y, core = place()
    j, s = lax.div(i, 2), lax.rem(i, 2)
    return jnp.where(core == 0, at(x, y - j, s), at(x - j, y, 1 - s))


def kv_request(i, k):
    x, y, core = place()
    j, s = lax.div(i, 2), lax.rem(i, 2)
    return jnp.where(core == s, at(x + k, y + j, 0), at(x + j, y + k, 1))


def source_at(n):
    return jnp.where(n < 4, 2 + lax.div(n, 2) + 4 * lax.rem(n, 2), jnp.where(n < 6, n, 7 - n))


def layer_kernel(
    zs, hist_ref, ids_ref, pattern_ref, gain_ref, kv_hbm, table_hbm, wq_hbm, wg_hbm, wo_hbm,
    recv_ref, out_ref,
    kv_ref, table_ref, wq_ref, wg_ref, wo_ref, wq_turned, pattern_in, patterns, plan, tables,
    stage, turn, parts, relay_in, parts_in, chunks, queries, gate, held, keys, acc, own, sums, sums_in,
    pieces, pieces_in,
    load_sem, plan_sem, pat_out, pat_in, pat_here, kv_out, kv_in, z1_out, z1_in, z2_out, z2_in, q_out, q_in, held_sem,
    o_out, o_in, z3_out, z3_in,
):
    z = lax.axis_index("item")
    rows, width = out_ref.shape
    part = width // zs
    heads = part // DH
    half = rows // 2
    peer_z = lambda d: lax.rem(z + d + zs, zs)

    barrier = pltpu.get_barrier_semaphore()
    for i in range(1, SOURCES):
        pl.semaphore_signal(barrier, inc=1, device_id={"cache": kv_source(i)}, device_id_type=MESH)
    for k in HOPS:
        pl.semaphore_signal(barrier, inc=1, device_id={"cache": ring_peer(k)}, device_id_type=MESH)
        pl.semaphore_signal(barrier, inc=1, device_id={"item": peer_z(k)}, device_id_type=MESH)

    loads = [
        pltpu.make_async_copy(src, dst, load_sem.at[n])
        for n, (src, dst) in enumerate(
            [(kv_hbm, kv_ref), (table_hbm, table_ref), (wq_hbm, wq_ref), (wg_hbm, wg_ref), (wo_hbm, wo_ref)]
        )
    ]
    for load in loads:
        load.start()

    listed = hist_ref[...]
    held_here = kv_hbm.shape[0]
    length = listed.shape[1]
    up_to = lax.broadcasted_iota(jnp.int32, (length, length), 0) <= lax.broadcasted_iota(
        jnp.int32, (length, length), 1
    )
    up_to = jnp.where(up_to, 1.0, 0.0)
    lane = lax.broadcasted_iota(jnp.int32, (SOURCES, plan.shape[2]), 1)
    row = lax.broadcasted_iota(jnp.int32, (SOURCES, 1), 0)
    me = lax.axis_index("cache")

    def count(found):
        return jnp.dot(jnp.where(found, 1.0, 0.0), up_to, preferred_element_type=jnp.float32)

    for g in range(listed.shape[0] // SOURCES):
        at_rows = slice(g * SOURCES, (g + 1) * SOURCES)
        some = listed[at_rows]
        found = lax.div(some, held_here) == me
        nth = count(found)
        table = jnp.zeros(lane.shape, jnp.int32)
        for slot in range(SLOT):
            block = jnp.where(found & (nth == slot + 1.0), some - me * held_here, 0)
            table = jnp.where(lane == slot, jnp.sum(block, axis=1, keepdims=True), table)
        plan[0, at_rows, :] = table
    source = jnp.zeros(row.shape, jnp.int32)
    for i in range(SOURCES):
        source = jnp.where(row == i, kv_source(i), source)
    for k in range(RING):
        request = me if k == 0 else ring_peer(k)
        some = jnp.broadcast_to(hist_ref[pl.ds(request, 1), :], (SOURCES, length))
        nth = count(lax.div(some, held_here) == source)
        table = jnp.zeros(lane.shape, jnp.int32)
        for slot in range(SLOT):
            spot = jnp.sum(jnp.where(nth <= slot, 1, 0), axis=1, keepdims=True)
            table = jnp.where(lane == slot, spot, table)
        plan[1, k * SOURCES : (k + 1) * SOURCES, :] = table
    plan_copy = pltpu.make_async_copy(plan, tables, plan_sem.at[0])
    plan_copy.start()

    to = lax.broadcasted_iota(jnp.int32, turn.shape, 0)
    of = lax.broadcasted_iota(jnp.int32, turn.shape, 1)
    turn[...] = jnp.where(
        of == lax.rem(to, BLK) * heads + lax.div(to, BLK), 1.0, 0.0
    ).astype(turn.dtype)

    def kv_copy(i, k):
        return pltpu.make_async_remote_copy(
            src_ref=stage.at[i, k],
            dst_ref=recv_ref.at[i, k],
            send_sem=kv_out.at[i * RING + k],
            recv_sem=kv_in.at[i * RING + k],
            device_id={"cache": kv_dest(i)},
            device_id_type=MESH,
        )

    def own_copy(k):
        return pltpu.make_async_copy(stage.at[0, k], recv_ref.at[0, k], kv_out.at[k])

    lead = SOURCES // 2

    def unit(u):
        group = lax.div(u + SOURCES - lead, SOURCES)
        k = jnp.where(group == 1, ORDER[1], jnp.where(group == 2, ORDER[2], ORDER[3]))
        k = jnp.where((group == 0) | (group == RING), 0, k)
        n = lax.rem(u + SOURCES - lead, SOURCES)
        n = jnp.where(group == 0, u, jnp.where(group == RING, u - (RING - 1) * SOURCES, n))
        return source_at(n), k

    def stage_unit(u):
        i, k = unit(u)
        request = kv_request(i, k)
        for slot in range(SLOT):
            block = kv_ref[tables[0, request, slot]]
            by_head = jnp.dot(turn[...], block, preferred_element_type=jnp.float32)
            turned = by_head.T.astype(stage.dtype)
            by_head = by_head.astype(stage.dtype)
            for p in range(heads // 2):
                stage[i, k, slot, p * BLK : (p + 1) * BLK, :] = jnp.concatenate(
                    [by_head[h * BLK : (h + 1) * BLK, :DH] for h in (2 * p, 2 * p + 1)], axis=1
                )
            for h in range(heads):
                first = heads // 2 * BLK + h * DH
                stage[i, k, slot, first : first + DH, :] = turned[DH:, h * BLK : (h + 1) * BLK]

    def send_unit(u):
        i, k = unit(u)

        @pl.when(i == 0)
        def _():
            own_copy(k).start()

        @pl.when(i != 0)
        def _():
            kv_copy(i, k).start()

    def each_unit(first, last, *does):
        def step(u, carry):
            for do in does:
                do(u)
            return carry

        lax.fori_loop(first, last, step, 0)

    def send_units(first, last):
        each_unit(first, last, stage_unit, send_unit)

    halves = {1: pl.ds(0, half), -1: pl.ds(half, half)}

    def z_remote(src, dst, out_sem, in_sem, d):
        return pltpu.make_async_remote_copy(
            src_ref=src, dst_ref=dst, send_sem=out_sem, recv_sem=in_sem,
            device_id={"item": peer_z(d)}, device_id_type=MESH,
        )

    def relay_copy(way):
        n = 0 if way == 1 else 1
        return z_remote(
            parts.at[2, halves[way]], relay_in.at[n], z1_out.at[n], z1_in.at[n], way
        )

    def part_copy(way, h):
        n = 0 if way == 1 else 1
        sem = 2 + 2 * n + (0 if h == 1 else 1)
        return z_remote(
            parts.at[way % zs, halves[h]], parts_in.at[n, halves[h]], z1_out.at[sem], z1_in.at[sem], way
        )

    def chunk_copy(way, h):
        n = (0 if way == 1 else 2) + (0 if h == 1 else 1)
        return z_remote(
            chunks.at[0, halves[h]], chunks.at[way % zs, halves[h]], z2_out.at[n], z2_in.at[n], way
        )

    def pass_copy(way):
        n = 4 if way == 1 else 5
        return z_remote(
            chunks.at[way % zs, halves[way]], chunks.at[2, halves[way]], z2_out.at[n], z2_in.at[n], way
        )

    def pattern_copy(k):
        return pltpu.make_async_remote_copy(
            src_ref=pattern_ref,
            dst_ref=pattern_in.at[k - 1],
            send_sem=pat_out.at[k - 1],
            recv_sem=pat_in.at[k - 1],
            device_id={"cache": ring_peer(-k)},
            device_id_type=MESH,
        )

    def pattern_here(k):
        src = pattern_ref if k == 0 else pattern_in.at[k - 1]
        return pltpu.make_async_copy(src, patterns.at[k], pat_here.at[k])

    def q_copy(k):
        return pltpu.make_async_remote_copy(
            src_ref=queries.at[0],
            dst_ref=queries.at[k],
            send_sem=q_out.at[k - 1],
            recv_sem=q_in.at[k - 1],
            device_id={"cache": ring_peer(-k)},
            device_id_type=MESH,
        )

    def o_copy(k):
        return pltpu.make_async_remote_copy(
            src_ref=sums.at[k - 1],
            dst_ref=sums_in.at[k - 1],
            send_sem=o_out.at[k - 1],
            recv_sem=o_in.at[k - 1],
            device_id={"cache": ring_peer(k)},
            device_id_type=MESH,
        )

    def z3_copy(i):
        return pltpu.make_async_remote_copy(
            src_ref=pieces.at[i],
            dst_ref=pieces_in.at[i - 1],
            send_sem=z3_out.at[i - 1],
            recv_sem=z3_in.at[i - 1],
            device_id={"item": peer_z(-i)},
            device_id_type=MESH,
        )

    pl.semaphore_wait(barrier, SOURCES - 1 + 2 * len(HOPS))

    for k in HOPS:
        pattern_copy(k).start()
    pattern_here(0).start()

    def pick(d):
        block = peer_z(d)
        ids = ids_ref[:, pl.ds(pl.multiple_of(block * rows, rows), rows)] - z * table_ref.shape[0]
        ids = jnp.broadcast_to(ids, (8, rows)).T[:, :1]
        hot = ids == lax.broadcasted_iota(jnp.int32, (rows, table_ref.shape[0]), 1)
        parts[d] = jnp.dot(
            jnp.where(hot, 1.0, 0.0).astype(table_ref.dtype),
            table_ref[...],
            preferred_element_type=jnp.float32,
        ).astype(parts.dtype)

    plan_copy.wait()
    loads[0].wait()
    send_units(0, 1)
    loads[1].wait()
    pick(2)
    relay_copy(1).start()
    relay_copy(-1).start()
    send_units(1, 2)
    pick(1)
    part_copy(1, -1).start()
    send_units(2, 3)
    pick(3)
    part_copy(-1, 1).start()
    send_units(3, 5)
    relay_copy(1).wait()
    parts[1, halves[1]] += relay_in[0]
    part_copy(1, 1).start()
    relay_copy(-1).wait()
    parts[3, halves[-1]] += relay_in[1]
    part_copy(-1, -1).start()
    pick(0)
    send_units(5, 9)
    for way in (1, -1):
        for h in (1, -1):
            part_copy(way, h).wait()
    chunks[0] = parts[0] + parts_in[0] + parts_in[1]
    for way in (1, -1):
        chunk_copy(way, way).start()
    for way in (1, -1):
        chunk_copy(way, -way).start()

    def silu(v):
        return v * jax.nn.sigmoid(v)

    for load in loads[2:]:
        load.wait()
    wq_turned[...] = wq_ref[...].astype(jnp.float32).T.astype(wq_turned.dtype)
    scale = 0.5 * DH ** (-0.5)

    def make_queries(d):
        queries[0, :, d * rows : (d + 1) * rows] = silu(
            lax.dot_general(
                wq_turned[...], chunks[d], (((1,), (1,)), ((), ())), preferred_element_type=jnp.float32
            )
        ).astype(queries.dtype) * jnp.asarray(scale, queries.dtype)

    make_queries(0)
    for way in (1, -1):
        chunk_copy(way, way).wait()
        pass_copy(way).start()
    send_units(9, AHEAD)
    each_unit(AHEAD, 20, stage_unit)
    for way in (1, -1):
        chunk_copy(way, -way).wait()
    make_queries(1)
    make_queries(3)
    each_unit(20, 28, stage_unit)
    for way in (1, -1):
        pass_copy(way).wait()
    make_queries(2)
    for k in HOPS:
        q_copy(k).start()
    each_unit(AHEAD, 28, send_unit)
    send_units(28, 32)
    gate[...] = silu(jnp.dot(chunks[0], wg_ref[...], preferred_element_type=jnp.float32))
    for k in HOPS:
        pattern_copy(k).wait()
        pattern_here(k).start()
    for k in range(RING):
        pattern_here(k).wait()

    def fetch(u):
        i, k = unit(u)
        return pltpu.make_async_copy(recv_ref.at[i, k], held.at[lax.rem(u, 2)], held_sem.at[lax.rem(u, 2)])

    def start_fetch(u):
        i, k = unit(u)

        @pl.when(i == 0)
        def _():
            own_copy(k).wait()

        @pl.when(i != 0)
        def _():
            kv_copy(i, k).wait_recv()

        fetch(u).start()

    units = SOURCES * RING
    own[...] = jnp.zeros_like(own)
    start_fetch(0)
    fetch(0).wait()

    def one_unit(u, carry):
        i, k = unit(u)

        n = lax.rem(u + SOURCES - lead, SOURCES)
        starts = (n == 0) | (u == 0)
        ends = (n == SOURCES - 1) | (u == units - 1)
        buf = lax.rem(u, 2)

        @pl.when(u + 1 < units)
        def _():
            start_fetch(u + 1)

        @pl.when(starts)
        def _():
            acc[...] = jnp.zeros_like(acc)

            @pl.when(k != 0)
            def _():
                q_copy(k).wait_recv()

        for slot in range(SLOT):
            at_slot = slice(slot * BLK, (slot + 1) * BLK)
            for p in range(heads // 2):
                pair = held[buf, slot, p * BLK : (p + 1) * BLK, :]
                keys[2 * p, at_slot, :] = pair[:, :DH]
                keys[2 * p + 1, at_slot, :] = pair[:, DH:]
        wanted = [[None] * SLOT for b in range(zs)]
        for slot in range(SLOT):
            spot = tables[1, k * SOURCES + i, slot]
            filled = jnp.where(spot < pattern_ref.shape[1], 1, 0)
            spot = jnp.minimum(spot, pattern_ref.shape[1] - 1)
            for b in range(zs):
                wish = patterns[k, peer_z(-b), spot] * filled
                wanted[b][slot] = wish.astype(jnp.float32).astype(keys.dtype)

        def half_scores(h, t):
            return jnp.dot(
                keys[h, t * STEP : (t + 1) * STEP, :],
                queries[k, h * DH : (h + 1) * DH, :],
                preferred_element_type=jnp.float32,
            )

        def add_values(h, t, weights):
            first = heads // 2 * BLK + h * DH
            slots = range(t * STEP // BLK, (t + 1) * STEP // BLK)
            values = [held[buf, slot, first : first + DH, :] for slot in slots]
            for b in range(zs):
                cols = slice(b * rows, (b + 1) * rows)
                masked = jnp.concatenate([v * wanted[b][s] for s, v in zip(slots, values)], axis=1)
                acc[h * DH : (h + 1) * DH, cols] += jnp.dot(
                    masked, weights[:, cols], preferred_element_type=jnp.float32
                )

        steps = [(h, t) for h in range(heads) for t in range(SLOT * BLK // STEP)]
        scores = half_scores(*steps[0])
        for m, (h, t) in enumerate(steps):
            later = half_scores(*steps[m + 1]) if m + 1 < len(steps) else None
            add_values(h, t, (scores + scores * jnp.tanh(scores)).astype(keys.dtype))
            scores = later

        @pl.when(ends & (k == 0))
        def _():
            own[...] += acc[...]

        @pl.when(ends & (k != 0))
        def _():
            sums[k - 1] = acc[...].astype(sums.dtype)
            o_copy(k).start()

        @pl.when(u + 1 < units)
        def _():
            fetch(u + 1).wait()

        return carry

    lax.fori_loop(0, units, one_unit, 0)

    for k in ORDER[1:]:
        o_copy(k).wait_recv()
    mine = None
    for i in HOPS + (0,):
        cols = slice(i * rows, (i + 1) * rows)
        total = own[:, cols]
        for k in ORDER[1:]:
            total += sums_in[k - 1, :, cols].astype(jnp.float32)
        total = total.T
        if i == 0:
            mine = total
        else:
            pieces[i] = total.astype(pieces.dtype)
            z3_copy(i).start()
    row_mean = jnp.sum(mine, axis=1, keepdims=True)
    row_square = jnp.sum(mine * mine, axis=1, keepdims=True)
    for i in (1, 3, 2):
        z3_copy(i).wait_recv()
        piece = pieces_in[i - 1].astype(jnp.float32)
        row_mean += jnp.sum(piece, axis=1, keepdims=True)
        row_square += jnp.sum(piece * piece, axis=1, keepdims=True)
    row_mean /= width
    row_square /= width
    norm = lax.rsqrt(row_square - row_mean * row_mean + norm_eps)
    total = chunks[0].astype(jnp.float32)
    for i in range(zs):
        a = mine if i == 0 else pieces_in[i - 1].astype(jnp.float32)
        cols = pl.ds(pl.multiple_of(peer_z(i) * part, part), part)
        hidden = (a - row_mean) * norm * gain_ref[:, cols] * gate[:, cols]
        total += jnp.dot(
            hidden.astype(jnp.bfloat16), wo_ref[cols, :], preferred_element_type=jnp.float32
        )
    out_ref[...] = total.astype(out_ref.dtype)

    for d in HOPS:
        z3_copy(d).wait_send()
        q_copy(d).wait_send()
        o_copy(d).wait_send()

    def drain(n, carry):
        kv_copy(lax.div(n, RING) + 1, lax.rem(n, RING)).wait_send()
        return carry

    lax.fori_loop(0, (SOURCES - 1) * RING, drain, 0)


def layer(zs, hist, ids, pattern, norm_gain, kv, table, w_query, w_gate, w_out):
    vmem = pl.BlockSpec(memory_space=pltpu.VMEM)
    hbm = pl.BlockSpec(memory_space=pl.ANY)
    cands = ids.shape[1]
    rows = cands // zs
    width = table.shape[1]
    part = w_query.shape[1]
    heads = part // DH
    kind = kv.dtype
    dma = pltpu.SemaphoreType.DMA
    moved = (SOURCES, RING, SLOT) + kv.shape[1:]
    return pl.pallas_call(
        functools.partial(layer_kernel, zs),
        out_shape=[jax.ShapeDtypeStruct(moved, kind), jax.ShapeDtypeStruct((rows, width), kind)],
        in_specs=[vmem] * 4 + [hbm] * 5,
        out_specs=[hbm, vmem],
        scratch_shapes=[
            pltpu.VMEM(kv.shape, kind),
            pltpu.VMEM(table.shape, kind),
            pltpu.VMEM(w_query.shape, kind),
            pltpu.VMEM(w_gate.shape, kind),
            pltpu.VMEM(w_out.shape, kind),
            pltpu.VMEM(w_query.shape[::-1], kind),
            pltpu.VMEM((RING - 1,) + pattern.shape, pattern.dtype),
            pltpu.SMEM((RING,) + pattern.shape, pattern.dtype),
            pltpu.VMEM((2, RING * SOURCES, 128), jnp.int32),
            pltpu.SMEM((2, RING * SOURCES, 128), jnp.int32),
            pltpu.VMEM(moved, kind),
            pltpu.VMEM((kv.shape[1], kv.shape[1]), kind),
            pltpu.VMEM((zs, rows, width), kind),
            pltpu.VMEM((2, rows // 2, width), kind),
            pltpu.VMEM((2, rows, width), kind),
            pltpu.VMEM((zs, rows, width), kind),
            pltpu.VMEM((RING, part, cands), kind),
            pltpu.VMEM((rows, width), jnp.float32),
            pltpu.VMEM((2, SLOT) + kv.shape[1:], kind),
            pltpu.VMEM((heads, SLOT * BLK, DH), kind),
            pltpu.VMEM((part, cands), jnp.float32),
            pltpu.VMEM((part, cands), jnp.float32),
            pltpu.VMEM((RING - 1, part, cands), kind),
            pltpu.VMEM((RING - 1, part, cands), kind),
            pltpu.VMEM((zs, rows, part), kind),
            pltpu.VMEM((zs - 1, rows, part), kind),
            dma((5,)),
            dma((1,)),
            dma((RING - 1,)),
            dma((RING - 1,)),
            dma((RING,)),
            dma((SOURCES * RING,)),
            dma((SOURCES * RING,)),
            dma((6,)),
            dma((6,)),
            dma((6,)),
            dma((6,)),
            dma((RING - 1,)),
            dma((RING - 1,)),
            dma((2,)),
            dma((RING - 1,)),
            dma((RING - 1,)),
            dma((zs - 1,)),
            dma((zs - 1,)),
        ],
        compiler_params=pltpu.CompilerParams(
            collective_id=0, has_side_effects=True, vmem_limit_bytes=62 * 2**20
        ),
        name="layer",
    )(hist, ids, pattern, norm_gain, kv, table, w_query, w_gate, w_out)[1]


def on_device(
    cand_items, item_table, kv_cache, hist_blocks, pattern, w_query, w_gate, norm_gain, w_out
):
    zs = lax.axis_size("item")
    out = layer(
        zs,
        hist_blocks,
        cand_items,
        pattern[0],
        norm_gain[None, :],
        kv_cache.reshape(kv_cache.shape[0], -1, kv_cache.shape[3]),
        item_table,
        w_query,
        w_gate,
        w_out,
    )
    return out[None]


def solution(mesh):
    placed = (
        P("cache", None),
        P("item", None),
        P("cache", None, "item", None),
        P(),
        P("cache", None, None),
        P(None, "item"),
        P(),
        P(),
        P(),
    )
    return jax.shard_map(
        on_device, mesh=mesh, in_specs=placed, out_specs=P("cache", "item", None), check_vma=False
    )
```

```python
import functools
import jax
import jax.numpy as jnp
from jax import lax
from jax.experimental import pallas as pl
from jax.experimental.pallas import tpu as pltpu
from jax.sharding import PartitionSpec as P

DH = 64
BLK = 128
SLOT = 4
CB = 256
RING = 4
SOURCES = 8
STEP = 256
AHEAD = 17
HOPS = (2, 1, 3)
ORDER = (0, 2, 1, 3)

norm_eps = 1e-05
MESH = pl.DeviceIdType.MESH


def at(x, y, core):
    return (lax.rem(x + 2 * RING, RING) * RING + lax.rem(y + 2 * RING, RING)) * 2 + core


def place():
    me = lax.axis_index("cache")
    core = lax.rem(me, 2)
    y = lax.rem(lax.div(me, 2), RING)
    x = lax.div(me, 2 * RING)
    return x, y, core


def ring_peer(k):
    x, y, core = place()
    return jnp.where(core == 0, at(x + k, y, 0), at(x, y + k, 1))


def kv_dest(i):
    x, y, core = place()
    j, s = lax.div(i, 2), lax.rem(i, 2)
    return jnp.where(core == s, at(x, y + j, 0), at(x + j, y, 1))


def kv_source(i):
    x, y, core = place()
    j, s = lax.div(i, 2), lax.rem(i, 2)
    return jnp.where(core == 0, at(x, y - j, s), at(x - j, y, 1 - s))


def kv_request(i, k):
    x, y, core = place()
    j, s = lax.div(i, 2), lax.rem(i, 2)
    return jnp.where(core == s, at(x + k, y + j, 0), at(x + j, y + k, 1))


def source_at(n):
    return jnp.where(n < 4, 2 + lax.div(n, 2) + 4 * lax.rem(n, 2), jnp.where(n < 6, n, 7 - n))


def layer_kernel(
    zs, hist_ref, ids_ref, pattern_ref, gain_ref, kv_hbm, table_hbm, wq_hbm, wg_hbm, wo_hbm,
    recv_ref, out_ref,
    kv_ref, table_ref, wq_ref, wg_ref, wo_ref, wq_turned, pattern_in, patterns, plan, tables,
    stage, turn, parts, relay_in, parts_in, chunks, queries, gate, held, keys, acc, own, sums, sums_in,
    pieces, pieces_in,
    load_sem, plan_sem, pat_out, pat_in, pat_here, kv_out, kv_in, z1_out, z1_in, z2_out, z2_in, q_out, q_in, held_sem,
    o_out, o_in, z3_out, z3_in,
):
    z = lax.axis_index("item")
    rows, width = out_ref.shape
    part = width // zs
    heads = part // DH
    half = rows // 2
    peer_z = lambda d: lax.rem(z + d + zs, zs)

    barrier = pltpu.get_barrier_semaphore()
    for i in range(1, SOURCES):
        pl.semaphore_signal(barrier, inc=1, device_id={"cache": kv_source(i)}, device_id_type=MESH)
    for k in HOPS:
        pl.semaphore_signal(barrier, inc=1, device_id={"cache": ring_peer(k)}, device_id_type=MESH)
        pl.semaphore_signal(barrier, inc=1, device_id={"item": peer_z(k)}, device_id_type=MESH)

    loads = [
        pltpu.make_async_copy(src, dst, load_sem.at[n])
        for n, (src, dst) in enumerate(
            [(kv_hbm, kv_ref), (table_hbm, table_ref), (wq_hbm, wq_ref), (wg_hbm, wg_ref), (wo_hbm, wo_ref)]
        )
    ]
    for load in loads:
        load.start()

    listed = hist_ref[...]
    held_here = kv_hbm.shape[0]
    length = listed.shape[1]
    up_to = lax.broadcasted_iota(jnp.int32, (length, length), 0) <= lax.broadcasted_iota(
        jnp.int32, (length, length), 1
    )
    up_to = jnp.where(up_to, 1.0, 0.0)
    lane = lax.broadcasted_iota(jnp.int32, (SOURCES, plan.shape[2]), 1)
    row = lax.broadcasted_iota(jnp.int32, (SOURCES, 1), 0)
    me = lax.axis_index("cache")

    def count(found):
        return jnp.dot(jnp.where(found, 1.0, 0.0), up_to, preferred_element_type=jnp.float32)

    for g in range(listed.shape[0] // SOURCES):
        at_rows = slice(g * SOURCES, (g + 1) * SOURCES)
        some = listed[at_rows]
        found = lax.div(some, held_here) == me
        nth = count(found)
        table = jnp.zeros(lane.shape, jnp.int32)
        for slot in range(SLOT):
            block = jnp.where(found & (nth == slot + 1.0), some - me * held_here, 0)
            table = jnp.where(lane == slot, jnp.sum(block, axis=1, keepdims=True), table)
        plan[0, at_rows, :] = table
    source = jnp.zeros(row.shape, jnp.int32)
    for i in range(SOURCES):
        source = jnp.where(row == i, kv_source(i), source)
    for k in range(RING):
        request = me if k == 0 else ring_peer(k)
        some = jnp.broadcast_to(hist_ref[pl.ds(request, 1), :], (SOURCES, length))
        nth = count(lax.div(some, held_here) == source)
        table = jnp.zeros(lane.shape, jnp.int32)
        for slot in range(SLOT):
            spot = jnp.sum(jnp.where(nth <= slot, 1, 0), axis=1, keepdims=True)
            table = jnp.where(lane == slot, spot, table)
        plan[1, k * SOURCES : (k + 1) * SOURCES, :] = table
    plan_copy = pltpu.make_async_copy(plan, tables, plan_sem.at[0])
    plan_copy.start()

    to = lax.broadcasted_iota(jnp.int32, turn.shape, 0)
    of = lax.broadcasted_iota(jnp.int32, turn.shape, 1)
    turn[...] = jnp.where(
        of == lax.rem(to, BLK) * heads + lax.div(to, BLK), 1.0, 0.0
    ).astype(turn.dtype)

    def kv_copy(i, k):
        return pltpu.make_async_remote_copy(
            src_ref=stage.at[i, k],
            dst_ref=recv_ref.at[i, k],
            send_sem=kv_out.at[i * RING + k],
            recv_sem=kv_in.at[i * RING + k],
            device_id={"cache": kv_dest(i)},
            device_id_type=MESH,
        )

    def own_copy(k):
        return pltpu.make_async_copy(stage.at[0, k], recv_ref.at[0, k], kv_out.at[k])

    lead = SOURCES // 2

    def unit(u):
        group = lax.div(u + SOURCES - lead, SOURCES)
        k = jnp.where(group == 1, ORDER[1], jnp.where(group == 2, ORDER[2], ORDER[3]))
        k = jnp.where((group == 0) | (group == RING), 0, k)
        n = lax.rem(u + SOURCES - lead, SOURCES)
        n = jnp.where(group == 0, u, jnp.where(group == RING, u - (RING - 1) * SOURCES, n))
        return source_at(n), k

    def stage_unit(u):
        i, k = unit(u)
        request = kv_request(i, k)
        for slot in range(SLOT):
            block = kv_ref[tables[0, request, slot]]
            by_head = jnp.dot(turn[...], block, preferred_element_type=jnp.float32)
            turned = by_head.T.astype(stage.dtype)
            by_head = by_head.astype(stage.dtype)
            for p in range(heads // 2):
                stage[i, k, slot, p * BLK : (p + 1) * BLK, :] = jnp.concatenate(
                    [by_head[h * BLK : (h + 1) * BLK, :DH] for h in (2 * p, 2 * p + 1)], axis=1
                )
            for h in range(heads):
                first = heads // 2 * BLK + h * DH
                stage[i, k, slot, first : first + DH, :] = turned[DH:, h * BLK : (h + 1) * BLK]

    def send_unit(u):
        i, k = unit(u)

        @pl.when(i == 0)
        def _():
            own_copy(k).start()

        @pl.when(i != 0)
        def _():
            kv_copy(i, k).start()

    def each_unit(first, last, *does):
        def step(u, carry):
            for do in does:
                do(u)
            return carry

        lax.fori_loop(first, last, step, 0)

    def send_units(first, last):
        each_unit(first, last, stage_unit, send_unit)

    halves = {1: pl.ds(0, half), -1: pl.ds(half, half)}

    def z_remote(src, dst, out_sem, in_sem, d):
        return pltpu.make_async_remote_copy(
            src_ref=src, dst_ref=dst, send_sem=out_sem, recv_sem=in_sem,
            device_id={"item": peer_z(d)}, device_id_type=MESH,
        )

    def relay_copy(way):
        n = 0 if way == 1 else 1
        return z_remote(
            parts.at[2, halves[way]], relay_in.at[n], z1_out.at[n], z1_in.at[n], way
        )

    def part_copy(way, h):
        n = 0 if way == 1 else 1
        sem = 2 + 2 * n + (0 if h == 1 else 1)
        return z_remote(
            parts.at[way % zs, halves[h]], parts_in.at[n, halves[h]], z1_out.at[sem], z1_in.at[sem], way
        )

    def chunk_copy(way, h):
        n = (0 if way == 1 else 2) + (0 if h == 1 else 1)
        return z_remote(
            chunks.at[0, halves[h]], chunks.at[way % zs, halves[h]], z2_out.at[n], z2_in.at[n], way
        )

    def pass_copy(way):
        n = 4 if way == 1 else 5
        return z_remote(
            chunks.at[way % zs, halves[way]], chunks.at[2, halves[way]], z2_out.at[n], z2_in.at[n], way
        )

    def pattern_copy(k):
        return pltpu.make_async_remote_copy(
            src_ref=pattern_ref,
            dst_ref=pattern_in.at[k - 1],
            send_sem=pat_out.at[k - 1],
            recv_sem=pat_in.at[k - 1],
            device_id={"cache": ring_peer(-k)},
            device_id_type=MESH,
        )

    def pattern_here(k):
        src = pattern_ref if k == 0 else pattern_in.at[k - 1]
        return pltpu.make_async_copy(src, patterns.at[k], pat_here.at[k])

    def q_copy(k, d):
        cols = pl.ds(d * rows, rows)
        return pltpu.make_async_remote_copy(
            src_ref=queries.at[0, :, cols],
            dst_ref=queries.at[k, :, cols],
            send_sem=q_out.at[d * (RING - 1) + k - 1],
            recv_sem=q_in.at[d * (RING - 1) + k - 1],
            device_id={"cache": ring_peer(-k)},
            device_id_type=MESH,
        )

    def o_copy(k):
        return pltpu.make_async_remote_copy(
            src_ref=sums.at[k - 1],
            dst_ref=sums_in.at[k - 1],
            send_sem=o_out.at[k - 1],
            recv_sem=o_in.at[k - 1],
            device_id={"cache": ring_peer(k)},
            device_id_type=MESH,
        )

    def z3_copy(i):
        return pltpu.make_async_remote_copy(
            src_ref=pieces.at[i],
            dst_ref=pieces_in.at[i - 1],
            send_sem=z3_out.at[i - 1],
            recv_sem=z3_in.at[i - 1],
            device_id={"item": peer_z(-i)},
            device_id_type=MESH,
        )

    pl.semaphore_wait(barrier, SOURCES - 1 + 2 * len(HOPS))

    for k in HOPS:
        pattern_copy(k).start()
    pattern_here(0).start()

    def pick(d):
        block = peer_z(d)
        ids = ids_ref[:, pl.ds(pl.multiple_of(block * rows, rows), rows)] - z * table_ref.shape[0]
        ids = jnp.broadcast_to(ids, (8, rows)).T[:, :1]
        hot = ids == lax.broadcasted_iota(jnp.int32, (rows, table_ref.shape[0]), 1)
        parts[d] = jnp.dot(
            jnp.where(hot, 1.0, 0.0).astype(table_ref.dtype),
            table_ref[...],
            preferred_element_type=jnp.float32,
        ).astype(parts.dtype)

    plan_copy.wait()
    loads[0].wait()
    send_units(0, 1)
    loads[1].wait()
    pick(2)
    relay_copy(1).start()
    relay_copy(-1).start()
    send_units(1, 2)
    pick(1)
    part_copy(1, -1).start()
    send_units(2, 3)
    pick(3)
    part_copy(-1, 1).start()
    send_units(3, 5)
    relay_copy(1).wait()
    parts[1, halves[1]] += relay_in[0]
    part_copy(1, 1).start()
    relay_copy(-1).wait()
    parts[3, halves[-1]] += relay_in[1]
    part_copy(-1, -1).start()
    pick(0)
    send_units(5, 9)
    for way in (1, -1):
        for h in (1, -1):
            part_copy(way, h).wait()
    chunks[0] = parts[0] + parts_in[0] + parts_in[1]
    for way in (1, -1):
        chunk_copy(way, way).start()
    for way in (1, -1):
        chunk_copy(way, -way).start()

    def silu(v):
        return v * jax.nn.sigmoid(v)

    for load in loads[2:]:
        load.wait()
    wq_turned[...] = wq_ref[...].astype(jnp.float32).T.astype(wq_turned.dtype)
    scale = 0.5 * DH ** (-0.5)

    def make_queries(d):
        queries[0, :, d * rows : (d + 1) * rows] = silu(
            lax.dot_general(
                wq_turned[...], chunks[d], (((1,), (1,)), ((), ())), preferred_element_type=jnp.float32
            )
        ).astype(queries.dtype) * jnp.asarray(scale, queries.dtype)
        for k in HOPS:
            q_copy(k, d).start()

    make_queries(0)
    for way in (1, -1):
        chunk_copy(way, way).wait()
        pass_copy(way).start()
    send_units(9, AHEAD)
    each_unit(AHEAD, 20, stage_unit)
    for way in (1, -1):
        chunk_copy(way, -way).wait()
    make_queries(1)
    make_queries(3)
    each_unit(20, 28, stage_unit)
    for way in (1, -1):
        pass_copy(way).wait()
    make_queries(2)
    each_unit(AHEAD, 28, send_unit)
    send_units(28, 32)
    gate[...] = silu(jnp.dot(chunks[0], wg_ref[...], preferred_element_type=jnp.float32))
    for k in HOPS:
        pattern_copy(k).wait()
        pattern_here(k).start()
    for k in range(RING):
        pattern_here(k).wait()

    def fetch(u):
        i, k = unit(u)
        return pltpu.make_async_copy(recv_ref.at[i, k], held.at[lax.rem(u, 2)], held_sem.at[lax.rem(u, 2)])

    def start_fetch(u):
        i, k = unit(u)

        @pl.when(i == 0)
        def _():
            own_copy(k).wait()

        @pl.when(i != 0)
        def _():
            kv_copy(i, k).wait_recv()

        fetch(u).start()

    units = SOURCES * RING
    own[...] = jnp.zeros_like(own)
    start_fetch(0)
    fetch(0).wait()

    def one_unit(u, carry):
        i, k = unit(u)

        n = lax.rem(u + SOURCES - lead, SOURCES)
        starts = (n == 0) | (u == 0)
        ends = (n == SOURCES - 1) | (u == units - 1)
        buf = lax.rem(u, 2)

        @pl.when(u + 1 < units)
        def _():
            start_fetch(u + 1)

        @pl.when(starts)
        def _():
            acc[...] = jnp.zeros_like(acc)

            @pl.when(k != 0)
            def _():
                for d in range(zs):
                    q_copy(k, d).wait_recv()

        for slot in range(SLOT):
            at_slot = slice(slot * BLK, (slot + 1) * BLK)
            for p in range(heads // 2):
                pair = held[buf, slot, p * BLK : (p + 1) * BLK, :]
                keys[2 * p, at_slot, :] = pair[:, :DH]
                keys[2 * p + 1, at_slot, :] = pair[:, DH:]
        wanted = [[None] * SLOT for b in range(zs)]
        for slot in range(SLOT):
            spot = tables[1, k * SOURCES + i, slot]
            filled = jnp.where(spot < pattern_ref.shape[1], 1, 0)
            spot = jnp.minimum(spot, pattern_ref.shape[1] - 1)
            for b in range(zs):
                wish = patterns[k, peer_z(-b), spot] * filled
                wanted[b][slot] = wish.astype(jnp.float32).astype(keys.dtype)

        def half_scores(h, t):
            return jnp.dot(
                keys[h, t * STEP : (t + 1) * STEP, :],
                queries[k, h * DH : (h + 1) * DH, :],
                preferred_element_type=jnp.float32,
            )

        def add_values(h, t, weights):
            first = heads // 2 * BLK + h * DH
            slots = range(t * STEP // BLK, (t + 1) * STEP // BLK)
            values = [held[buf, slot, first : first + DH, :] for slot in slots]
            for b in range(zs):
                cols = slice(b * rows, (b + 1) * rows)
                masked = jnp.concatenate([v * wanted[b][s] for s, v in zip(slots, values)], axis=1)
                acc[h * DH : (h + 1) * DH, cols] += jnp.dot(
                    masked, weights[:, cols], preferred_element_type=jnp.float32
                )

        steps = [(h, t) for h in range(heads) for t in range(SLOT * BLK // STEP)]
        scores = half_scores(*steps[0])
        for m, (h, t) in enumerate(steps):
            later = half_scores(*steps[m + 1]) if m + 1 < len(steps) else None
            add_values(h, t, (scores + scores * jnp.tanh(scores)).astype(keys.dtype))
            scores = later

        @pl.when(ends & (k == 0))
        def _():
            own[...] += acc[...]

        @pl.when(ends & (k != 0))
        def _():
            sums[k - 1] = acc[...].astype(sums.dtype)
            o_copy(k).start()

        @pl.when(u + 1 < units)
        def _():
            fetch(u + 1).wait()

        return carry

    lax.fori_loop(0, units, one_unit, 0)

    for k in ORDER[1:]:
        o_copy(k).wait_recv()
    mine = None
    for i in HOPS + (0,):
        cols = slice(i * rows, (i + 1) * rows)
        total = own[:, cols]
        for k in ORDER[1:]:
            total += sums_in[k - 1, :, cols].astype(jnp.float32)
        total = total.T
        if i == 0:
            mine = total
        else:
            pieces[i] = total.astype(pieces.dtype)
            z3_copy(i).start()
    row_mean = jnp.sum(mine, axis=1, keepdims=True)
    row_square = jnp.sum(mine * mine, axis=1, keepdims=True)
    for i in (1, 3, 2):
        z3_copy(i).wait_recv()
        piece = pieces_in[i - 1].astype(jnp.float32)
        row_mean += jnp.sum(piece, axis=1, keepdims=True)
        row_square += jnp.sum(piece * piece, axis=1, keepdims=True)
    row_mean /= width
    row_square /= width
    norm = lax.rsqrt(row_square - row_mean * row_mean + norm_eps)
    total = chunks[0].astype(jnp.float32)
    for i in range(zs):
        a = mine if i == 0 else pieces_in[i - 1].astype(jnp.float32)
        cols = pl.ds(pl.multiple_of(peer_z(i) * part, part), part)
        hidden = (a - row_mean) * norm * gain_ref[:, cols] * gate[:, cols]
        total += jnp.dot(
            hidden.astype(jnp.bfloat16), wo_ref[cols, :], preferred_element_type=jnp.float32
        )
    out_ref[...] = total.astype(out_ref.dtype)

    for d in HOPS:
        z3_copy(d).wait_send()
        for c in range(zs):
            q_copy(d, c).wait_send()
        o_copy(d).wait_send()

    def drain(n, carry):
        kv_copy(lax.div(n, RING) + 1, lax.rem(n, RING)).wait_send()
        return carry

    lax.fori_loop(0, (SOURCES - 1) * RING, drain, 0)


def layer(zs, hist, ids, pattern, norm_gain, kv, table, w_query, w_gate, w_out):
    vmem = pl.BlockSpec(memory_space=pltpu.VMEM)
    hbm = pl.BlockSpec(memory_space=pl.ANY)
    cands = ids.shape[1]
    rows = cands // zs
    width = table.shape[1]
    part = w_query.shape[1]
    heads = part // DH
    kind = kv.dtype
    dma = pltpu.SemaphoreType.DMA
    moved = (SOURCES, RING, SLOT) + kv.shape[1:]
    return pl.pallas_call(
        functools.partial(layer_kernel, zs),
        out_shape=[jax.ShapeDtypeStruct(moved, kind), jax.ShapeDtypeStruct((rows, width), kind)],
        in_specs=[vmem] * 4 + [hbm] * 5,
        out_specs=[hbm, vmem],
        scratch_shapes=[
            pltpu.VMEM(kv.shape, kind),
            pltpu.VMEM(table.shape, kind),
            pltpu.VMEM(w_query.shape, kind),
            pltpu.VMEM(w_gate.shape, kind),
            pltpu.VMEM(w_out.shape, kind),
            pltpu.VMEM(w_query.shape[::-1], kind),
            pltpu.VMEM((RING - 1,) + pattern.shape, pattern.dtype),
            pltpu.SMEM((RING,) + pattern.shape, pattern.dtype),
            pltpu.VMEM((2, RING * SOURCES, 128), jnp.int32),
            pltpu.SMEM((2, RING * SOURCES, 128), jnp.int32),
            pltpu.VMEM(moved, kind),
            pltpu.VMEM((kv.shape[1], kv.shape[1]), kind),
            pltpu.VMEM((zs, rows, width), kind),
            pltpu.VMEM((2, rows // 2, width), kind),
            pltpu.VMEM((2, rows, width), kind),
            pltpu.VMEM((zs, rows, width), kind),
            pltpu.VMEM((RING, part, cands), kind),
            pltpu.VMEM((rows, width), jnp.float32),
            pltpu.VMEM((2, SLOT) + kv.shape[1:], kind),
            pltpu.VMEM((heads, SLOT * BLK, DH), kind),
            pltpu.VMEM((part, cands), jnp.float32),
            pltpu.VMEM((part, cands), jnp.float32),
            pltpu.VMEM((RING - 1, part, cands), kind),
            pltpu.VMEM((RING - 1, part, cands), kind),
            pltpu.VMEM((zs, rows, part), kind),
            pltpu.VMEM((zs - 1, rows, part), kind),
            dma((5,)),
            dma((1,)),
            dma((RING - 1,)),
            dma((RING - 1,)),
            dma((RING,)),
            dma((SOURCES * RING,)),
            dma((SOURCES * RING,)),
            dma((6,)),
            dma((6,)),
            dma((6,)),
            dma((6,)),
            dma((zs * (RING - 1),)),
            dma((zs * (RING - 1),)),
            dma((2,)),
            dma((RING - 1,)),
            dma((RING - 1,)),
            dma((zs - 1,)),
            dma((zs - 1,)),
        ],
        compiler_params=pltpu.CompilerParams(
            collective_id=0, has_side_effects=True, vmem_limit_bytes=62 * 2**20
        ),
        name="layer",
    )(hist, ids, pattern, norm_gain, kv, table, w_query, w_gate, w_out)[1]


def on_device(
    cand_items, item_table, kv_cache, hist_blocks, pattern, w_query, w_gate, norm_gain, w_out
):
    zs = lax.axis_size("item")
    out = layer(
        zs,
        hist_blocks,
        cand_items,
        pattern[0],
        norm_gain[None, :],
        kv_cache.reshape(kv_cache.shape[0], -1, kv_cache.shape[3]),
        item_table,
        w_query,
        w_gate,
        w_out,
    )
    return out[None]


def solution(mesh):
    placed = (
        P("cache", None),
        P("item", None),
        P("cache", None, "item", None),
        P(),
        P("cache", None, None),
        P(None, "item"),
        P(),
        P(),
        P(),
    )
    return jax.shard_map(
        on_device, mesh=mesh, in_specs=placed, out_specs=P("cache", "item", None), check_vma=False
    )
```
